32 devices in a mesh: groups: 2 (over y), blk: 8 (over z, x), pair: 2 (over core).
Axes of the slice: x: 2, y: 2, z: 4, core: 2. Of those that a mesh axis runs over, the one named last changes fastest.
Arguments:
- embeddings: bfloat16 [8192, 768], P(('groups', 'blk', 'pair')), parts along dimension 0, may hold values from -24 to 24
- cluster_ids: int32 [8192], P(('groups', 'blk', 'pair')), parts along dimension 0, may hold values from 0 to 7, as said below
Outputs:
- scores: float32 [8192], P(('groups', 'blk', 'pair')), parts along dimension 0
The draws below stay inside these ranges and needn't reach their ends.
There are 2 independent parts, one for each index of `groups`. The reference program is written for one: setup_inputs(seed, part) draws one part's arguments, and reference() takes and returns one part's arrays. A program takes and returns all parts, laid end to end along the dimension named above; each array names one. Nothing has to cross between parts.
Inputs may be any that keep to these rules, and one draw needn't show every extreme that they name: `cluster_ids`: within the 256 rows of one device each cluster id occurs either not at all or exactly 64 times, and one cluster id occurs in the rows of every device.
All inputs are finite; a program needn't handle non-finite values.
Results may differ from the reference program's by a relative error of at most 0.0003.
Values may be sent and summed in bfloat16 or wider, within the bound.
No kernel may reach another device: no remote copies, remote signals or barrier semaphores. Data moves between devices by JAX's collectives and lax.ppermute only.
A program may use at most 64 MiB of HBM per device.

```python
import math
import jax
import jax.numpy as jnp
from jax import lax

D = 768
ROWS_DEV = 256
CLUSTERS = 8
CAP = 64
ROWS = 4096
N_PAIR = 2


def shuffle_row(row_key, labels):
    return jax.random.permutation(row_key, labels)


def cluster_plan(key):
    sources = ROWS // ROWS_DEV
    root_random_key, favor_key, noise_key, shuffle_key = jax.random.split(key, 4)
    labels = jnp.arange(CLUSTERS, dtype=jnp.int32)
    weights = jax.random.randint(root_random_key, (CLUSTERS,), 0, 4, dtype=jnp.int32) * 64
    favored = jax.random.randint(favor_key, (), 0, CLUSTERS, dtype=jnp.int32)
    weights = jnp.where(labels == favored, 100000, weights)
    noise = jax.random.randint(noise_key, (sources, CLUSTERS), 0, 192, dtype=jnp.int32)
    ranking = (weights[None, :] + noise) * CLUSTERS + labels[None, :]
    order = jnp.argsort(-ranking, axis=1)
    chosen = order[:, :CLUSTERS // 2].astype(jnp.int32)
    filled = jnp.repeat(chosen, CAP, axis=1)
    row_keys = jax.random.split(shuffle_key, sources)
    mixed = jax.vmap(shuffle_row)(row_keys, filled)
    return mixed.reshape(ROWS).astype(jnp.int32)


def shared_direction(root_random_key, twin_index):
    return jax.random.truncated_normal(jax.random.fold_in(root_random_key, twin_index), -5.0, 5.0, (D,), jnp.float32)


def draw_cluster_ids(key, part):
    labels = cluster_plan(key)
    return labels


def draw_embeddings(key, part):
    labels = cluster_plan(key)
    key = jax.random.fold_in(key, 7)
    center_key = jax.random.fold_in(key, 0)
    align_key = jax.random.fold_in(key, 1)
    noise_key = jax.random.fold_in(key, 2)
    scale_key = jax.random.fold_in(key, 3)
    twin_key = jax.random.fold_in(key, 5)
    flag_key = jax.random.fold_in(key, 6)
    code_key = jax.random.fold_in(key, 7)
    jitter_key = jax.random.fold_in(key, 8)
    root = math.sqrt(D)
    centers = jax.random.truncated_normal(center_key, -5.0, 5.0, (CLUSTERS, D), jnp.float32) / root
    align = jax.random.uniform(align_key, (ROWS, 1), jnp.float32, 0.3, 1.2)
    twin_groups = max(1, ROWS // CLUSTERS // 48)
    flagged = jax.random.randint(flag_key, (ROWS, 1), 0, 16, dtype=jnp.int32) == 0
    codes = jax.random.randint(code_key, (ROWS,), 0, twin_groups, dtype=jnp.int32)
    paired_index_list = labels * twin_groups + codes
    twin_dirs = jax.vmap(lambda twin_index: shared_direction(twin_key, twin_index))(paired_index_list) / root
    jitter = jax.random.truncated_normal(jitter_key, -5.0, 5.0, (ROWS, D), jnp.float32) / root
    twin_part = 0.3 * centers[labels] + twin_dirs + 0.08 * jitter
    noise = jax.random.truncated_normal(noise_key, -5.0, 5.0, (ROWS, D), jnp.float32) / root
    scale = jnp.exp(jax.random.uniform(scale_key, (ROWS, 1), jnp.float32, math.log(0.5), math.log(4.0)))
    bulk = align * centers[labels] + noise
    values = scale * jnp.where(flagged, twin_part, bulk)
    return values.astype(jnp.bfloat16)


def setup_inputs(seed: int = 0, part: int = 0) -> dict:
    seeds = jax.random.split(jax.random.key(seed), 3)
    part_splits = jax.random.split(jax.random.fold_in(seeds[2], part), 3)
    return {
        "embeddings": draw_embeddings(jax.random.fold_in(jax.random.fold_in(seeds[2], part), 71), part),
        "cluster_ids": draw_cluster_ids(jax.random.fold_in(jax.random.fold_in(seeds[2], part), 71), part),
    }


def unit_vectors(values):
    widened = values.astype(jnp.float32)
    scale = lax.rsqrt(lax.optimization_barrier(jnp.sum(widened * widened, axis=1, keepdims=True)) + 1e-06)
    return (widened * scale).astype(jnp.bfloat16)

def reference(embeddings, cluster_ids):
    units = unit_vectors(embeddings)
    largest = 2 * ROWS_DEV * N_PAIR
    positions = jnp.arange(largest, dtype=jnp.int32)

    def one_cluster(label):
        inside = cluster_ids == label
        members = jnp.nonzero(inside, size=largest, fill_value=0)[0].astype(jnp.int32)
        member_count = jnp.sum(inside.astype(jnp.int32))
        living = positions < member_count
        selected_rows = units[members]
        similarity_matrix = jnp.dot(selected_rows, selected_rows.T, preferred_element_type=jnp.float32)
        keeping = living[None, :] & (positions[:, None] != positions[None, :])
        density = lax.optimization_barrier(jnp.sum(jnp.where(keeping, jnp.exp(similarity_matrix * 10.0), 0.0), axis=1))
        values = jnp.where(living, jnp.log(jnp.where(living, density, 1.0)), 0.0)
        return (members, values)
    members, values = lax.map(one_cluster, jnp.arange(CLUSTERS, dtype=jnp.int32))
    return jnp.zeros((ROWS,), jnp.float32).at[members.reshape(-1)].add(values.reshape(-1))
```

```python
import functools

import jax
import jax.numpy as jnp
from jax import lax
from jax.experimental import pallas as pl
from jax.experimental.pallas import tpu as pltpu
from jax.sharding import PartitionSpec as P

SHARPNESS = 10.0
EPSILON = 1e-06
EMPTY_MARK = 2.0
EMPTY_ABOVE = 1.5
DIRECT_OWNERS = 8


def vmem(count):
    return [pl.BlockSpec(memory_space=pltpu.VMEM)] * count


def params(mib=24):
    return pltpu.CompilerParams(vmem_limit_bytes=mib * 1024 * 1024)


def prepare_kernel(owners, capacity, me_ref, rows_ref, ids_ref, *outs):
    block_refs, pick_ref = outs[:-1], outs[-1]
    me = me_ref[0]
    row_count, width = rows_ref.shape
    values = rows_ref[...].astype(jnp.float32)
    scale = lax.rsqrt(jnp.sum(values * values, axis=1, keepdims=True) + EPSILON)
    units = (values * scale).astype(jnp.bfloat16)
    relative = jnp.reshape(ids_ref[...], (1, row_count)) ^ me
    labels = lax.broadcasted_iota(jnp.int32, (owners, row_count), 0)
    inside = (labels == relative).astype(jnp.float32)
    above = lax.broadcasted_iota(jnp.int32, (row_count, row_count), 0)
    right = lax.broadcasted_iota(jnp.int32, (row_count, row_count), 1)
    earlier = jnp.where(above < right, 1.0, 0.0).astype(jnp.bfloat16)
    before = jnp.dot(inside.astype(jnp.bfloat16), earlier, preferred_element_type=jnp.float32)
    rank = jnp.sum(before * inside, axis=0, keepdims=True).astype(jnp.int32)
    slot = relative * capacity + rank
    slots = owners * capacity
    pick = jnp.where(lax.broadcasted_iota(jnp.int32, (slots, row_count), 0) == slot, 1.0, 0.0).astype(
        jnp.bfloat16
    )
    pick_ref[...] = pick
    counts = jnp.sum(inside, axis=1, keepdims=True)
    first = lax.broadcasted_iota(jnp.int32, (capacity, 128), 1) == 0
    for k, block_ref in enumerate(block_refs):
        block = jnp.dot(
            pick[k * capacity:(k + 1) * capacity], units, preferred_element_type=jnp.float32
        ).astype(jnp.bfloat16)
        block_ref[...] = block
        empty = counts[k:k + 1] == 0.0
        block_ref[:, 0:128] = jnp.where(
            first & empty, EMPTY_MARK, block[:, 0:128].astype(jnp.float32)
        ).astype(jnp.bfloat16)


def prepare(me, rows, ids, owners, capacity):
    row_count, width = rows.shape
    shapes = [jax.ShapeDtypeStruct((capacity, width), jnp.bfloat16)] * owners
    shapes.append(jax.ShapeDtypeStruct((owners * capacity, row_count), jnp.bfloat16))
    return pl.pallas_call(
        functools.partial(prepare_kernel, owners, capacity),
        out_shape=shapes,
        in_specs=[pl.BlockSpec(memory_space=pltpu.SMEM)] + vmem(2),
        out_specs=vmem(len(shapes)),
        compiler_params=params(),
    )(me, rows, ids)


def partial_sums(own, others, others_refs, own_block):
    capacity = others_refs[0].shape[0]
    count = own.shape[0]
    total = jnp.zeros((1, count), jnp.float32)
    products = lax.dot_general(others, own, (((1,), (1,)), ((), ())), preferred_element_type=jnp.float32)
    for k, block_ref in enumerate(others_refs):
        powers = jnp.exp(products[k * capacity:(k + 1) * capacity] * SHARPNESS)
        if own_block:
            row = lax.broadcasted_iota(jnp.int32, powers.shape, 0) + k * capacity
            powers = jnp.where(row == lax.broadcasted_iota(jnp.int32, powers.shape, 1), 0.0, powers)
        living = block_ref[0:1, 0:1].astype(jnp.float32) < EMPTY_ABOVE
        total = total + jnp.where(living, jnp.sum(powers, axis=0, keepdims=True), 0.0)
    return total


def own_kernel(owners, *refs):
    block_refs, joined_ref, total_ref = refs[:owners], refs[owners], refs[owners + 1]
    capacity = block_refs[0].shape[0]
    for k, block_ref in enumerate(block_refs):
        joined_ref[k * capacity:(k + 1) * capacity, :] = block_ref[...]
    own = joined_ref[...]
    total_ref[...] = partial_sums(own, own, block_refs, True)


def own_sums(blocks):
    capacity, width = blocks[0].shape
    slots = len(blocks) * capacity
    return pl.pallas_call(
        functools.partial(own_kernel, len(blocks)),
        out_shape=[
            jax.ShapeDtypeStruct((slots, width), jnp.bfloat16),
            jax.ShapeDtypeStruct((1, slots), jnp.float32),
        ],
        in_specs=vmem(len(blocks)),
        out_specs=vmem(2),
        compiler_params=params(),
        cost_estimate=pl.CostEstimate(
            flops=2 * slots * slots * width, bytes_accessed=4 * slots * width, transcendentals=slots * slots
        ),
    )(*blocks)


def cross_kernel(owners, *refs):
    block_refs, joined_ref, total_ref = refs[:owners], refs[owners], refs[owners + 1]
    score_refs = refs[owners + 2:2 * owners + 2]
    others_ref = refs[-1]
    capacity = block_refs[0].shape[0]
    for k, block_ref in enumerate(block_refs):
        others_ref[k * capacity:(k + 1) * capacity, :] = block_ref[...]
    total = total_ref[...] + partial_sums(joined_ref[...], others_ref[...], block_refs, False)
    scores = jnp.log(jnp.where(total > 0.0, total, 1.0))
    for k, score_ref in enumerate(score_refs):
        score_ref[...] = scores[:, k * capacity:(k + 1) * capacity]


def cross_scores(blocks, joined, total):
    capacity, width = blocks[0].shape
    slots = len(blocks) * capacity
    return pl.pallas_call(
        functools.partial(cross_kernel, len(blocks)),
        out_shape=[jax.ShapeDtypeStruct((1, capacity), jnp.float32)] * len(blocks),
        in_specs=vmem(len(blocks) + 2),
        out_specs=vmem(len(blocks)),
        scratch_shapes=[pltpu.VMEM((slots, width), jnp.bfloat16)],
        compiler_params=params(),
    )(*blocks, joined, total)


def collect_kernel(owners, *refs):
    score_refs, pick_ref, out_ref = refs[:owners], refs[owners], refs[owners + 1]
    scores = jnp.concatenate([score_ref[...] for score_ref in score_refs], axis=1)
    high = scores.astype(jnp.bfloat16)
    rest = scores - high.astype(jnp.float32)
    middle = rest.astype(jnp.bfloat16)
    low = (rest - middle.astype(jnp.float32)).astype(jnp.bfloat16)
    pick = pick_ref[...]
    parts = [jnp.dot(part, pick, preferred_element_type=jnp.float32) for part in (high, middle, low)]
    out_ref[...] = jnp.reshape((parts[0] + parts[1]) + parts[2], out_ref.shape)


def collect(scores, pick):
    return pl.pallas_call(
        functools.partial(collect_kernel, len(scores)),
        out_shape=jax.ShapeDtypeStruct((pick.shape[1],), jnp.float32),
        in_specs=vmem(len(scores) + 1),
        out_specs=pl.BlockSpec(memory_space=pltpu.VMEM),
        compiler_params=params(),
    )(*scores, pick)


def swap(block, axis, step, size):
    if step == 0:
        return block
    return lax.ppermute(block, axis, [(i, i ^ step) for i in range(size)])


def direct_shards(embeddings, cluster_ids):
    owners = lax.axis_size("blk")
    capacity = 2 * embeddings.shape[0] // owners
    me = jnp.reshape(lax.axis_index("blk").astype(jnp.int32), (1,))
    *blocks, pick = prepare(me, embeddings, cluster_ids, owners, capacity)
    own_blocks = [None] * owners
    for k in reversed(range(owners)):
        own_blocks[k] = swap(blocks[k], "blk", k, owners)
    other_blocks = [swap(block, "pair", 1, 2) for block in own_blocks]
    joined, total = own_sums(own_blocks)
    scores = cross_scores(other_blocks, joined, total)
    returned = [swap(scores[k], "blk", k, owners) for k in range(owners)]
    return collect(returned, pick)


def unit_vectors(values):
    widened = values.astype(jnp.float32)
    scale = lax.rsqrt(jnp.sum(widened * widened, axis=1, keepdims=True) + EPSILON)
    return (widened * scale).astype(jnp.bfloat16)


def wide_shards(embeddings, cluster_ids):
    row_count, width = embeddings.shape
    owners = lax.axis_size("blk")
    capacity = 2 * row_count // owners
    slots = owners * capacity
    units = unit_vectors(embeddings)
    marks = (cluster_ids[:, None] == jnp.arange(owners, dtype=jnp.int32)[None, :]).astype(jnp.bfloat16)
    row_order = jnp.arange(row_count, dtype=jnp.int32)
    earlier = (row_order[:, None] > row_order[None, :]).astype(jnp.bfloat16)
    before = jnp.dot(earlier, marks, preferred_element_type=jnp.float32)
    rank = jnp.sum(before * marks.astype(jnp.float32), axis=1).astype(jnp.int32)
    target = cluster_ids * capacity + rank
    empty_row = jnp.where(jnp.arange(width) == 0, EMPTY_MARK, 0.0).astype(jnp.bfloat16)
    send = jnp.broadcast_to(empty_row[None, :], (slots, width)).at[target].set(units)
    own = lax.all_to_all(
        send.reshape(owners, capacity, width), "blk", split_axis=0, concat_axis=0, tiled=True
    ).reshape(slots, width)
    other = lax.ppermute(own, "pair", [(0, 1), (1, 0)])
    columns = jnp.concatenate([own, other], axis=0)
    living = columns[:, 0].astype(jnp.float32) < EMPTY_ABOVE
    products = lax.dot_general(own, columns, (((1,), (1,)), ((), ())), preferred_element_type=jnp.float32)
    position = jnp.arange(2 * slots, dtype=jnp.int32)
    keep = living[None, :] & (position[:slots, None] != position[None, :])
    density = jnp.sum(jnp.where(keep, jnp.exp(products * SHARPNESS), 0.0), axis=1)
    scores = jnp.log(jnp.where(living[:slots], density, 1.0)).reshape(owners, capacity)
    returned = lax.all_to_all(scores, "blk", split_axis=0, concat_axis=0, tiled=True)
    return returned.reshape(slots)[target]


def solution(mesh):
    placed = (P(("groups", "blk", "pair"), None), P(("groups", "blk", "pair")))
    shards = direct_shards if mesh.shape["blk"] <= DIRECT_OWNERS else wide_shards
    return jax.shard_map(
        shards, mesh=mesh, in_specs=placed, out_specs=P(("groups", "blk", "pair")), check_vma=False
    )
```

```python
import functools

import jax
import jax.numpy as jnp
from jax import lax
from jax.experimental import pallas as pl
from jax.experimental.pallas import tpu as pltpu
from jax.sharding import PartitionSpec as P

SHARPNESS = 10.0
EPSILON = 1e-06
EMPTY_MARK = 2.0
EMPTY_ABOVE = 1.5
DIRECT_OWNERS = 8
SCORE_LANES = 128


def vmem(count):
    return [pl.BlockSpec(memory_space=pltpu.VMEM)] * count


def params(mib=24):
    return pltpu.CompilerParams(vmem_limit_bytes=mib * 1024 * 1024)


def prepare_kernel(owners, capacity, me_ref, rows_ref, ids_ref, *outs):
    block_refs, pick_ref = outs[:-1], outs[-1]
    me = me_ref[0]
    row_count, width = rows_ref.shape
    values = rows_ref[...].astype(jnp.float32)
    scale = lax.rsqrt(jnp.sum(values * values, axis=1, keepdims=True) + EPSILON)
    units = (values * scale).astype(jnp.bfloat16)
    relative = jnp.reshape(ids_ref[...], (1, row_count)) ^ me
    labels = lax.broadcasted_iota(jnp.int32, (owners, row_count), 0)
    inside = (labels == relative).astype(jnp.float32)
    above = lax.broadcasted_iota(jnp.int32, (row_count, row_count), 0)
    right = lax.broadcasted_iota(jnp.int32, (row_count, row_count), 1)
    earlier = jnp.where(above < right, 1.0, 0.0).astype(jnp.bfloat16)
    before = jnp.dot(inside.astype(jnp.bfloat16), earlier, preferred_element_type=jnp.float32)
    rank = jnp.sum(before * inside, axis=0, keepdims=True).astype(jnp.int32)
    slot = relative * capacity + rank
    slots = owners * capacity
    pick = jnp.where(lax.broadcasted_iota(jnp.int32, (slots, row_count), 0) == slot, 1.0, 0.0).astype(
        jnp.bfloat16
    )
    pick_ref[...] = pick
    counts = jnp.sum(inside, axis=1, keepdims=True)
    first = lax.broadcasted_iota(jnp.int32, (capacity, 128), 1) == 0
    for k, block_ref in enumerate(block_refs):
        block = jnp.dot(
            pick[k * capacity:(k + 1) * capacity], units, preferred_element_type=jnp.float32
        ).astype(jnp.bfloat16)
        block_ref[...] = block
        empty = counts[k:k + 1] == 0.0
        block_ref[:, 0:128] = jnp.where(
            first & empty, EMPTY_MARK, block[:, 0:128].astype(jnp.float32)
        ).astype(jnp.bfloat16)


def prepare(me, rows, ids, owners, capacity):
    row_count, width = rows.shape
    shapes = [jax.ShapeDtypeStruct((capacity, width), jnp.bfloat16)] * owners
    shapes.append(jax.ShapeDtypeStruct((owners * capacity, row_count), jnp.bfloat16))
    return pl.pallas_call(
        functools.partial(prepare_kernel, owners, capacity),
        out_shape=shapes,
        in_specs=[pl.BlockSpec(memory_space=pltpu.SMEM)] + vmem(2),
        out_specs=vmem(len(shapes)),
        compiler_params=params(),
    )(me, rows, ids)


def partial_sums(own, others, others_refs, own_block):
    capacity = others_refs[0].shape[0]
    count = own.shape[0]
    total = jnp.zeros((1, count), jnp.float32)
    products = lax.dot_general(others, own, (((1,), (1,)), ((), ())), preferred_element_type=jnp.float32)
    for k, block_ref in enumerate(others_refs):
        powers = jnp.exp(products[k * capacity:(k + 1) * capacity] * SHARPNESS)
        if own_block:
            row = lax.broadcasted_iota(jnp.int32, powers.shape, 0) + k * capacity
            powers = jnp.where(row == lax.broadcasted_iota(jnp.int32, powers.shape, 1), 0.0, powers)
        living = block_ref[0:1, 0:1].astype(jnp.float32) < EMPTY_ABOVE
        total = total + jnp.where(living, jnp.sum(powers, axis=0, keepdims=True), 0.0)
    return total


def own_kernel(owners, *refs):
    block_refs, joined_ref, total_ref = refs[:owners], refs[owners], refs[owners + 1]
    capacity = block_refs[0].shape[0]
    for k, block_ref in enumerate(block_refs):
        joined_ref[k * capacity:(k + 1) * capacity, :] = block_ref[...]
    own = joined_ref[...]
    total_ref[...] = partial_sums(own, own, block_refs, True)


def own_sums(blocks):
    capacity, width = blocks[0].shape
    slots = len(blocks) * capacity
    return pl.pallas_call(
        functools.partial(own_kernel, len(blocks)),
        out_shape=[
            jax.ShapeDtypeStruct((slots, width), jnp.bfloat16),
            jax.ShapeDtypeStruct((1, slots), jnp.float32),
        ],
        in_specs=vmem(len(blocks)),
        out_specs=vmem(2),
        compiler_params=params(),
        cost_estimate=pl.CostEstimate(
            flops=2 * slots * slots * width, bytes_accessed=4 * slots * width, transcendentals=slots * slots
        ),
    )(*blocks)


def cross_kernel(owners, me_ref, *refs):
    block_refs, joined_ref, total_ref, score_ref, others_ref = refs[:owners], *refs[owners:]
    me = me_ref[0]
    capacity = block_refs[0].shape[0]
    for k, block_ref in enumerate(block_refs):
        others_ref[k * capacity:(k + 1) * capacity, :] = block_ref[...]
    total = total_ref[...] + partial_sums(joined_ref[...], others_ref[...], block_refs, False)
    scores = jnp.log(jnp.where(total > 0.0, total, 1.0))
    for k in range(owners):
        score_ref[pl.ds(me ^ k, 1), 0:capacity] = scores[:, k * capacity:(k + 1) * capacity]


def cross_scores(me, blocks, joined, total):
    capacity, width = blocks[0].shape
    slots = len(blocks) * capacity
    return pl.pallas_call(
        functools.partial(cross_kernel, len(blocks)),
        out_shape=jax.ShapeDtypeStruct((len(blocks), SCORE_LANES), jnp.float32),
        in_specs=[pl.BlockSpec(memory_space=pltpu.SMEM)] + vmem(len(blocks) + 2),
        out_specs=pl.BlockSpec(memory_space=pltpu.VMEM),
        scratch_shapes=[pltpu.VMEM((slots, width), jnp.bfloat16)],
        compiler_params=params(),
    )(me, *blocks, joined, total)


def collect_kernel(capacity, me_ref, score_ref, pick_ref, out_ref):
    me = me_ref[0]
    scores = jnp.concatenate(
        [score_ref[pl.ds(me ^ k, 1), 0:capacity] for k in range(score_ref.shape[0])], axis=1
    )
    high = scores.astype(jnp.bfloat16)
    rest = scores - high.astype(jnp.float32)
    middle = rest.astype(jnp.bfloat16)
    low = (rest - middle.astype(jnp.float32)).astype(jnp.bfloat16)
    pick = pick_ref[...]
    parts = [jnp.dot(part, pick, preferred_element_type=jnp.float32) for part in (high, middle, low)]
    out_ref[...] = jnp.reshape((parts[0] + parts[1]) + parts[2], out_ref.shape)


def collect(me, scores, pick, capacity):
    return pl.pallas_call(
        functools.partial(collect_kernel, capacity),
        out_shape=jax.ShapeDtypeStruct((pick.shape[1],), jnp.float32),
        in_specs=[pl.BlockSpec(memory_space=pltpu.SMEM)] + vmem(2),
        out_specs=pl.BlockSpec(memory_space=pltpu.VMEM),
        compiler_params=params(),
    )(me, scores, pick)


def swap(block, axis, step, size):
    if step == 0:
        return block
    return lax.ppermute(block, axis, [(i, i ^ step) for i in range(size)])


def direct_shards(embeddings, cluster_ids):
    owners = lax.axis_size("blk")
    capacity = 2 * embeddings.shape[0] // owners
    me = jnp.reshape(lax.axis_index("blk").astype(jnp.int32), (1,))
    *blocks, pick = prepare(me, embeddings, cluster_ids, owners, capacity)
    own_blocks = [None] * owners
    for k in reversed(range(owners)):
        own_blocks[k] = swap(blocks[k], "blk", k, owners)
    other_blocks = [swap(block, "pair", 1, 2) for block in own_blocks]
    joined, total = own_sums(own_blocks)
    scores = cross_scores(me, other_blocks, joined, total)
    returned = lax.all_to_all(scores, "blk", split_axis=0, concat_axis=0, tiled=True)
    return collect(me, returned, pick, capacity)


def unit_vectors(values):
    widened = values.astype(jnp.float32)
    scale = lax.rsqrt(jnp.sum(widened * widened, axis=1, keepdims=True) + EPSILON)
    return (widened * scale).astype(jnp.bfloat16)


def wide_shards(embeddings, cluster_ids):
    row_count, width = embeddings.shape
    owners = lax.axis_size("blk")
    capacity = 2 * row_count // owners
    slots = owners * capacity
    units = unit_vectors(embeddings)
    marks = (cluster_ids[:, None] == jnp.arange(owners, dtype=jnp.int32)[None, :]).astype(jnp.bfloat16)
    row_order = jnp.arange(row_count, dtype=jnp.int32)
    earlier = (row_order[:, None] > row_order[None, :]).astype(jnp.bfloat16)
    before = jnp.dot(earlier, marks, preferred_element_type=jnp.float32)
    rank = jnp.sum(before * marks.astype(jnp.float32), axis=1).astype(jnp.int32)
    target = cluster_ids * capacity + rank
    empty_row = jnp.where(jnp.arange(width) == 0, EMPTY_MARK, 0.0).astype(jnp.bfloat16)
    send = jnp.broadcast_to(empty_row[None, :], (slots, width)).at[target].set(units)
    own = lax.all_to_all(
        send.reshape(owners, capacity, width), "blk", split_axis=0, concat_axis=0, tiled=True
    ).reshape(slots, width)
    other = lax.ppermute(own, "pair", [(0, 1), (1, 0)])
    columns = jnp.concatenate([own, other], axis=0)
    living = columns[:, 0].astype(jnp.float32) < EMPTY_ABOVE
    products = lax.dot_general(own, columns, (((1,), (1,)), ((), ())), preferred_element_type=jnp.float32)
    position = jnp.arange(2 * slots, dtype=jnp.int32)
    keep = living[None, :] & (position[:slots, None] != position[None, :])
    density = jnp.sum(jnp.where(keep, jnp.exp(products * SHARPNESS), 0.0), axis=1)
    scores = jnp.log(jnp.where(living[:slots], density, 1.0)).reshape(owners, capacity)
    returned = lax.all_to_all(scores, "blk", split_axis=0, concat_axis=0, tiled=True)
    return returned.reshape(slots)[target]


def solution(mesh):
    placed = (P(("groups", "blk", "pair"), None), P(("groups", "blk", "pair")))
    shards = direct_shards if mesh.shape["blk"] <= DIRECT_OWNERS else wide_shards
    return jax.shard_map(
        shards, mesh=mesh, in_specs=placed, out_specs=P(("groups", "blk", "pair")), check_vma=False
    )
```

```python
import functools

import jax
import jax.numpy as jnp
from jax import lax
from jax.experimental import pallas as pl
from jax.experimental.pallas import tpu as pltpu
from jax.sharding import PartitionSpec as P

SHARPNESS = 10.0
EPSILON = 1e-06
EMPTY_MARK = 2.0
EMPTY_ABOVE = 1.5
DIRECT_OWNERS = 8
SCORE_LANES = 128


def vmem(count):
    return [pl.BlockSpec(memory_space=pltpu.VMEM)] * count


def params(mib=24):
    return pltpu.CompilerParams(vmem_limit_bytes=mib * 1024 * 1024)


def pick_kernel(owners, capacity, me_ref, ids_ref, pick_ref, empty_ref):
    row_count = ids_ref.shape[0]
    step = jnp.reshape(ids_ref[...], (1, row_count)) ^ me_ref[0]
    relative = sum(jnp.where(step == value, k, 0) for k, value in enumerate(steps_of(owners)))
    labels = lax.broadcasted_iota(jnp.int32, (owners, row_count), 0)
    inside = (labels == relative).astype(jnp.float32)
    above = lax.broadcasted_iota(jnp.int32, (row_count, row_count), 0)
    right = lax.broadcasted_iota(jnp.int32, (row_count, row_count), 1)
    earlier = jnp.where(above < right, 1.0, 0.0).astype(jnp.bfloat16)
    before = jnp.dot(inside.astype(jnp.bfloat16), earlier, preferred_element_type=jnp.float32)
    rank = jnp.sum(before * inside, axis=0, keepdims=True).astype(jnp.int32)
    slot = relative * capacity + rank
    slots = owners * capacity
    pick_ref[...] = jnp.where(
        lax.broadcasted_iota(jnp.int32, (slots, row_count), 0) == slot, 1.0, 0.0
    ).astype(jnp.bfloat16)
    counts = jnp.broadcast_to(jnp.sum(inside, axis=1, keepdims=True), empty_ref.shape)
    first = lax.broadcasted_iota(jnp.int32, empty_ref.shape, 1) == 0
    empty_ref[...] = jnp.where(first & (counts == 0.0), EMPTY_MARK, 0.0)


def prepare_kernel(owners, capacity, rows_ref, pick_ref, empty_ref, *block_refs):
    values = rows_ref[...].astype(jnp.float32)
    scale = lax.rsqrt(jnp.sum(values * values, axis=1, keepdims=True) + EPSILON)
    units = (values * scale).astype(jnp.bfloat16)
    for k, block_ref in enumerate(block_refs):
        block = jnp.dot(
            pick_ref[k * capacity:(k + 1) * capacity, :], units, preferred_element_type=jnp.float32
        )
        block_ref[...] = block.astype(jnp.bfloat16)
        block_ref[:, 0:128] = (block[:, 0:128] + empty_ref[k:k + 1, :]).astype(jnp.bfloat16)


def prepare(me, rows, ids, owners, capacity):
    row_count, width = rows.shape
    pick, empty = pl.pallas_call(
        functools.partial(pick_kernel, owners, capacity),
        out_shape=[
            jax.ShapeDtypeStruct((owners * capacity, row_count), jnp.bfloat16),
            jax.ShapeDtypeStruct((owners, 128), jnp.float32),
        ],
        in_specs=[pl.BlockSpec(memory_space=pltpu.SMEM)] + vmem(1),
        out_specs=vmem(2),
        compiler_params=params(),
    )(me, ids)
    blocks = pl.pallas_call(
        functools.partial(prepare_kernel, owners, capacity),
        out_shape=[jax.ShapeDtypeStruct((capacity, width), jnp.bfloat16)] * owners,
        in_specs=vmem(3),
        out_specs=vmem(owners),
        compiler_params=params(),
    )(rows, pick, empty)
    return blocks, pick


def partial_sums(own, others, others_refs, own_block):
    capacity = others_refs[0].shape[0]
    count = own.shape[0]
    total = jnp.zeros((1, count), jnp.float32)
    products = lax.dot_general(others, own, (((1,), (1,)), ((), ())), preferred_element_type=jnp.float32)
    for k, block_ref in enumerate(others_refs):
        powers = jnp.exp(products[k * capacity:(k + 1) * capacity] * SHARPNESS)
        if own_block:
            row = lax.broadcasted_iota(jnp.int32, powers.shape, 0) + k * capacity
            powers = jnp.where(row == lax.broadcasted_iota(jnp.int32, powers.shape, 1), 0.0, powers)
        living = block_ref[0:1, 0:1].astype(jnp.float32) < EMPTY_ABOVE
        total = total + jnp.where(living, jnp.sum(powers, axis=0, keepdims=True), 0.0)
    return total


def own_kernel(owners, *refs):
    block_refs, joined_ref, total_ref = refs[:owners], refs[owners], refs[owners + 1]
    capacity = block_refs[0].shape[0]
    for k, block_ref in enumerate(block_refs):
        joined_ref[k * capacity:(k + 1) * capacity, :] = block_ref[...]
    own = joined_ref[...]
    total_ref[...] = partial_sums(own, own, block_refs, True)


def own_sums(blocks):
    capacity, width = blocks[0].shape
    slots = len(blocks) * capacity
    return pl.pallas_call(
        functools.partial(own_kernel, len(blocks)),
        out_shape=[
            jax.ShapeDtypeStruct((slots, width), jnp.bfloat16),
            jax.ShapeDtypeStruct((1, slots), jnp.float32),
        ],
        in_specs=vmem(len(blocks)),
        out_specs=vmem(2),
        compiler_params=params(),
        cost_estimate=pl.CostEstimate(
            flops=2 * slots * slots * width, bytes_accessed=4 * slots * width, transcendentals=slots * slots
        ),
    )(*blocks)


def cross_kernel(owners, me_ref, *refs):
    block_refs, joined_ref, total_ref, score_ref, others_ref = refs[:owners], *refs[owners:]
    me = me_ref[0]
    capacity = block_refs[0].shape[0]
    for k, block_ref in enumerate(block_refs):
        others_ref[k * capacity:(k + 1) * capacity, :] = block_ref[...]
    total = total_ref[...] + partial_sums(joined_ref[...], others_ref[...], block_refs, False)
    scores = jnp.log(jnp.where(total > 0.0, total, 1.0))
    for k, step in enumerate(steps_of(owners)):
        score_ref[pl.ds(me ^ step, 1), 0:capacity] = scores[:, k * capacity:(k + 1) * capacity]


def cross_scores(me, blocks, joined, total):
    capacity, width = blocks[0].shape
    slots = len(blocks) * capacity
    return pl.pallas_call(
        functools.partial(cross_kernel, len(blocks)),
        out_shape=jax.ShapeDtypeStruct((len(blocks), SCORE_LANES), jnp.float32),
        in_specs=[pl.BlockSpec(memory_space=pltpu.SMEM)] + vmem(len(blocks) + 2),
        out_specs=pl.BlockSpec(memory_space=pltpu.VMEM),
        scratch_shapes=[pltpu.VMEM((slots, width), jnp.bfloat16)],
        compiler_params=params(),
    )(me, *blocks, joined, total)


def collect_kernel(capacity, me_ref, score_ref, pick_ref, out_ref):
    me = me_ref[0]
    scores = jnp.concatenate(
        [score_ref[pl.ds(me ^ step, 1), 0:capacity] for step in steps_of(score_ref.shape[0])], axis=1
    )
    high = scores.astype(jnp.bfloat16)
    rest = scores - high.astype(jnp.float32)
    middle = rest.astype(jnp.bfloat16)
    low = (rest - middle.astype(jnp.float32)).astype(jnp.bfloat16)
    parts = jnp.dot(
        jnp.concatenate([high, middle, low], axis=0), pick_ref[...], preferred_element_type=jnp.float32
    )
    out_ref[...] = jnp.reshape((parts[0:1] + parts[1:2]) + parts[2:3], out_ref.shape)


def collect(me, scores, pick, capacity):
    return pl.pallas_call(
        functools.partial(collect_kernel, capacity),
        out_shape=jax.ShapeDtypeStruct((pick.shape[1],), jnp.float32),
        in_specs=[pl.BlockSpec(memory_space=pltpu.SMEM)] + vmem(2),
        out_specs=pl.BlockSpec(memory_space=pltpu.VMEM),
        compiler_params=params(),
    )(me, scores, pick)


def steps_of(owners):
    if owners == 8:
        return (0, 6, 5, 7, 3, 1, 2, 4)
    return tuple(range(owners))


def swap(block, axis, step, size):
    if step == 0:
        return block
    return lax.ppermute(block, axis, [(i, i ^ step) for i in range(size)])


def direct_shards(embeddings, cluster_ids):
    owners = lax.axis_size("blk")
    capacity = 2 * embeddings.shape[0] // owners
    me = jnp.reshape(lax.axis_index("blk").astype(jnp.int32), (1,))
    blocks, pick = prepare(me, embeddings, cluster_ids, owners, capacity)
    own_blocks = [None] * owners
    for k, step in enumerate(steps_of(owners)):
        own_blocks[k] = swap(blocks[k], "blk", step, owners)
    other_blocks = [swap(block, "pair", 1, 2) for block in own_blocks]
    joined, total = own_sums(own_blocks)
    scores = cross_scores(me, other_blocks, joined, total)
    returned = lax.all_to_all(scores, "blk", split_axis=0, concat_axis=0, tiled=True)
    return collect(me, returned, pick, capacity)


def unit_vectors(values):
    widened = values.astype(jnp.float32)
    scale = lax.rsqrt(jnp.sum(widened * widened, axis=1, keepdims=True) + EPSILON)
    return (widened * scale).astype(jnp.bfloat16)


def wide_shards(embeddings, cluster_ids):
    row_count, width = embeddings.shape
    owners = lax.axis_size("blk")
    capacity = 2 * row_count // owners
    slots = owners * capacity
    units = unit_vectors(embeddings)
    marks = (cluster_ids[:, None] == jnp.arange(owners, dtype=jnp.int32)[None, :]).astype(jnp.bfloat16)
    row_order = jnp.arange(row_count, dtype=jnp.int32)
    earlier = (row_order[:, None] > row_order[None, :]).astype(jnp.bfloat16)
    before = jnp.dot(earlier, marks, preferred_element_type=jnp.float32)
    rank = jnp.sum(before * marks.astype(jnp.float32), axis=1).astype(jnp.int32)
    target = cluster_ids * capacity + rank
    empty_row = jnp.where(jnp.arange(width) == 0, EMPTY_MARK, 0.0).astype(jnp.bfloat16)
    send = jnp.broadcast_to(empty_row[None, :], (slots, width)).at[target].set(units)
    own = lax.all_to_all(
        send.reshape(owners, capacity, width), "blk", split_axis=0, concat_axis=0, tiled=True
    ).reshape(slots, width)
    other = lax.ppermute(own, "pair", [(0, 1), (1, 0)])
    columns = jnp.concatenate([own, other], axis=0)
    living = columns[:, 0].astype(jnp.float32) < EMPTY_ABOVE
    products = lax.dot_general(own, columns, (((1,), (1,)), ((), ())), preferred_element_type=jnp.float32)
    position = jnp.arange(2 * slots, dtype=jnp.int32)
    keep = living[None, :] & (position[:slots, None] != position[None, :])
    density = jnp.sum(jnp.where(keep, jnp.exp(products * SHARPNESS), 0.0), axis=1)
    scores = jnp.log(jnp.where(living[:slots], density, 1.0)).reshape(owners, capacity)
    returned = lax.all_to_all(scores, "blk", split_axis=0, concat_axis=0, tiled=True)
    return returned.reshape(slots)[target]


def solution(mesh):
    placed = (P(("groups", "blk", "pair"), None), P(("groups", "blk", "pair")))
    shards = direct_shards if mesh.shape["blk"] <= DIRECT_OWNERS else wide_shards
    return jax.shard_map(
        shards, mesh=mesh, in_specs=placed, out_specs=P(("groups", "blk", "pair")), check_vma=False
    )
```

```python
import functools

import jax
import jax.numpy as jnp
from jax import lax
from jax.experimental import pallas as pl
from jax.experimental.pallas import tpu as pltpu
from jax.sharding import PartitionSpec as P

SHARPNESS = 10.0
EPSILON = 1e-06
EMPTY_MARK = 2.0
EMPTY_ABOVE = 1.5
DIRECT_OWNERS = 8
SCORE_LANES = 128


def vmem(count):
    return [pl.BlockSpec(memory_space=pltpu.VMEM)] * count


def params(mib=24):
    return pltpu.CompilerParams(vmem_limit_bytes=mib * 1024 * 1024)


def prepare_kernel(owners, capacity, me_ref, rows_hbm, ids_hbm, *refs):
    block_refs = refs[:owners]
    pick_ref, rows_ref, ids_ref, sems = refs[owners:]
    ids_copy = pltpu.make_async_copy(ids_hbm, ids_ref, sems.at[0])
    rows_copy = pltpu.make_async_copy(rows_hbm, rows_ref, sems.at[1])
    ids_copy.start()
    rows_copy.start()
    row_count = ids_ref.shape[0]
    above = lax.broadcasted_iota(jnp.int32, (row_count, row_count), 0)
    right = lax.broadcasted_iota(jnp.int32, (row_count, row_count), 1)
    earlier = jnp.where(above < right, 1.0, 0.0).astype(jnp.bfloat16)
    labels = lax.broadcasted_iota(jnp.int32, (owners, row_count), 0)
    ids_copy.wait()
    step = jnp.reshape(ids_ref[...], (1, row_count)) ^ me_ref[0]
    relative = sum(jnp.where(step == value, k, 0) for k, value in enumerate(steps_of(owners)))
    inside = (labels == relative).astype(jnp.float32)
    before = jnp.dot(inside.astype(jnp.bfloat16), earlier, preferred_element_type=jnp.float32)
    rank = jnp.sum(before * inside, axis=0, keepdims=True).astype(jnp.int32)
    slot = relative * capacity + rank
    slots = owners * capacity
    pick_ref[...] = jnp.where(
        lax.broadcasted_iota(jnp.int32, (slots, row_count), 0) == slot, 1.0, 0.0
    ).astype(jnp.bfloat16)
    counts = jnp.broadcast_to(jnp.sum(inside, axis=1, keepdims=True), (owners, 128))
    first = lax.broadcasted_iota(jnp.int32, (owners, 128), 1) == 0
    marks = jnp.where(first & (counts == 0.0), EMPTY_MARK, 0.0)
    rows_copy.wait()
    values = rows_ref[...].astype(jnp.float32)
    scale = lax.rsqrt(jnp.sum(values * values, axis=1, keepdims=True) + EPSILON)
    units = (values * scale).astype(jnp.bfloat16)
    for k, block_ref in enumerate(block_refs):
        block = jnp.dot(
            pick_ref[k * capacity:(k + 1) * capacity, :], units, preferred_element_type=jnp.float32
        )
        block_ref[...] = block.astype(jnp.bfloat16)
        block_ref[:, 0:128] = (block[:, 0:128] + marks[k:k + 1, :]).astype(jnp.bfloat16)


def prepare(me, rows, ids, owners, capacity):
    row_count, width = rows.shape
    *blocks, pick = pl.pallas_call(
        functools.partial(prepare_kernel, owners, capacity),
        out_shape=[jax.ShapeDtypeStruct((capacity, width), jnp.bfloat16)] * owners
        + [jax.ShapeDtypeStruct((owners * capacity, row_count), jnp.bfloat16)],
        in_specs=[pl.BlockSpec(memory_space=pltpu.SMEM)] + [pl.BlockSpec(memory_space=pltpu.HBM)] * 2,
        out_specs=vmem(owners + 1),
        scratch_shapes=[
            pltpu.VMEM(rows.shape, rows.dtype),
            pltpu.VMEM(ids.shape, ids.dtype),
            pltpu.SemaphoreType.DMA((2,)),
        ],
        compiler_params=params(),
    )(
        me,
        pltpu.with_memory_space_constraint(rows, pltpu.HBM),
        pltpu.with_memory_space_constraint(ids, pltpu.HBM),
    )
    return blocks, pick


def partial_sums(own, others, others_refs, own_block):
    capacity = others_refs[0].shape[0]
    count = own.shape[0]
    total = jnp.zeros((1, count), jnp.float32)
    products = lax.dot_general(others, own, (((1,), (1,)), ((), ())), preferred_element_type=jnp.float32)
    for k, block_ref in enumerate(others_refs):
        powers = jnp.exp(products[k * capacity:(k + 1) * capacity] * SHARPNESS)
        if own_block:
            row = lax.broadcasted_iota(jnp.int32, powers.shape, 0) + k * capacity
            powers = jnp.where(row == lax.broadcasted_iota(jnp.int32, powers.shape, 1), 0.0, powers)
        living = block_ref[0:1, 0:1].astype(jnp.float32) < EMPTY_ABOVE
        total = total + jnp.where(living, jnp.sum(powers, axis=0, keepdims=True), 0.0)
    return total


def own_kernel(owners, *refs):
    block_refs, joined_ref, total_ref = refs[:owners], refs[owners], refs[owners + 1]
    capacity = block_refs[0].shape[0]
    for k, block_ref in enumerate(block_refs):
        joined_ref[k * capacity:(k + 1) * capacity, :] = block_ref[...]
    own = joined_ref[...]
    total_ref[...] = partial_sums(own, own, block_refs, True)


def own_sums(blocks):
    capacity, width = blocks[0].shape
    slots = len(blocks) * capacity
    return pl.pallas_call(
        functools.partial(own_kernel, len(blocks)),
        out_shape=[
            jax.ShapeDtypeStruct((slots, width), jnp.bfloat16),
            jax.ShapeDtypeStruct((1, slots), jnp.float32),
        ],
        in_specs=vmem(len(blocks)),
        out_specs=vmem(2),
        compiler_params=params(),
        cost_estimate=pl.CostEstimate(
            flops=2 * slots * slots * width, bytes_accessed=4 * slots * width, transcendentals=slots * slots
        ),
    )(*blocks)


def cross_kernel(owners, me_ref, *refs):
    block_refs, joined_ref, total_ref, score_ref, others_ref = refs[:owners], *refs[owners:]
    me = me_ref[0]
    capacity = block_refs[0].shape[0]
    for k, block_ref in enumerate(block_refs):
        others_ref[k * capacity:(k + 1) * capacity, :] = block_ref[...]
    total = total_ref[...] + partial_sums(joined_ref[...], others_ref[...], block_refs, False)
    scores = jnp.log(jnp.where(total > 0.0, total, 1.0))
    for k, step in enumerate(steps_of(owners)):
        score_ref[pl.ds(me ^ step, 1), 0:capacity] = scores[:, k * capacity:(k + 1) * capacity]


def cross_scores(me, blocks, joined, total):
    capacity, width = blocks[0].shape
    slots = len(blocks) * capacity
    return pl.pallas_call(
        functools.partial(cross_kernel, len(blocks)),
        out_shape=jax.ShapeDtypeStruct((len(blocks), SCORE_LANES), jnp.float32),
        in_specs=[pl.BlockSpec(memory_space=pltpu.SMEM)] + vmem(len(blocks) + 2),
        out_specs=pl.BlockSpec(memory_space=pltpu.VMEM),
        scratch_shapes=[pltpu.VMEM((slots, width), jnp.bfloat16)],
        compiler_params=params(),
    )(me, *blocks, joined, total)


def collect_kernel(capacity, me_ref, score_ref, pick_ref, out_ref):
    me = me_ref[0]
    scores = jnp.concatenate(
        [score_ref[pl.ds(me ^ step, 1), 0:capacity] for step in steps_of(score_ref.shape[0])], axis=1
    )
    high = scores.astype(jnp.bfloat16)
    rest = scores - high.astype(jnp.float32)
    middle = rest.astype(jnp.bfloat16)
    low = (rest - middle.astype(jnp.float32)).astype(jnp.bfloat16)
    parts = jnp.dot(
        jnp.concatenate([high, middle, low], axis=0), pick_ref[...], preferred_element_type=jnp.float32
    )
    out_ref[...] = jnp.reshape((parts[0:1] + parts[1:2]) + parts[2:3], out_ref.shape)


def collect(me, scores, pick, capacity):
    return pl.pallas_call(
        functools.partial(collect_kernel, capacity),
        out_shape=jax.ShapeDtypeStruct((pick.shape[1],), jnp.float32),
        in_specs=[pl.BlockSpec(memory_space=pltpu.SMEM)] + vmem(2),
        out_specs=pl.BlockSpec(memory_space=pltpu.VMEM),
        compiler_params=params(),
    )(me, scores, pick)


def steps_of(owners):
    if owners == 8:
        return (0, 6, 5, 7, 3, 1, 2, 4)
    return tuple(range(owners))


def swap(block, axis, step, size):
    if step == 0:
        return block
    return lax.ppermute(block, axis, [(i, i ^ step) for i in range(size)])


def direct_shards(embeddings, cluster_ids):
    owners = lax.axis_size("blk")
    capacity = 2 * embeddings.shape[0] // owners
    me = jnp.reshape(lax.axis_index("blk").astype(jnp.int32), (1,))
    blocks, pick = prepare(me, embeddings, cluster_ids, owners, capacity)
    own_blocks = [None] * owners
    for k, step in enumerate(steps_of(owners)):
        own_blocks[k] = swap(blocks[k], "blk", step, owners)
    other_blocks = [swap(block, "pair", 1, 2) for block in own_blocks]
    joined, total = own_sums(own_blocks)
    scores = cross_scores(me, other_blocks, joined, total)
    returned = lax.all_to_all(scores, "blk", split_axis=0, concat_axis=0, tiled=True)
    return collect(me, returned, pick, capacity)


def unit_vectors(values):
    widened = values.astype(jnp.float32)
    scale = lax.rsqrt(jnp.sum(widened * widened, axis=1, keepdims=True) + EPSILON)
    return (widened * scale).astype(jnp.bfloat16)


def wide_shards(embeddings, cluster_ids):
    row_count, width = embeddings.shape
    owners = lax.axis_size("blk")
    capacity = 2 * row_count // owners
    slots = owners * capacity
    units = unit_vectors(embeddings)
    marks = (cluster_ids[:, None] == jnp.arange(owners, dtype=jnp.int32)[None, :]).astype(jnp.bfloat16)
    row_order = jnp.arange(row_count, dtype=jnp.int32)
    earlier = (row_order[:, None] > row_order[None, :]).astype(jnp.bfloat16)
    before = jnp.dot(earlier, marks, preferred_element_type=jnp.float32)
    rank = jnp.sum(before * marks.astype(jnp.float32), axis=1).astype(jnp.int32)
    target = cluster_ids * capacity + rank
    empty_row = jnp.where(jnp.arange(width) == 0, EMPTY_MARK, 0.0).astype(jnp.bfloat16)
    send = jnp.broadcast_to(empty_row[None, :], (slots, width)).at[target].set(units)
    own = lax.all_to_all(
        send.reshape(owners, capacity, width), "blk", split_axis=0, concat_axis=0, tiled=True
    ).reshape(slots, width)
    other = lax.ppermute(own, "pair", [(0, 1), (1, 0)])
    columns = jnp.concatenate([own, other], axis=0)
    living = columns[:, 0].astype(jnp.float32) < EMPTY_ABOVE
    products = lax.dot_general(own, columns, (((1,), (1,)), ((), ())), preferred_element_type=jnp.float32)
    position = jnp.arange(2 * slots, dtype=jnp.int32)
    keep = living[None, :] & (position[:slots, None] != position[None, :])
    density = jnp.sum(jnp.where(keep, jnp.exp(products * SHARPNESS), 0.0), axis=1)
    scores = jnp.log(jnp.where(living[:slots], density, 1.0)).reshape(owners, capacity)
    returned = lax.all_to_all(scores, "blk", split_axis=0, concat_axis=0, tiled=True)
    return returned.reshape(slots)[target]


def solution(mesh):
    placed = (P(("groups", "blk", "pair"), None), P(("groups", "blk", "pair")))
    shards = direct_shards if mesh.shape["blk"] <= DIRECT_OWNERS else wide_shards
    return jax.shard_map(
        shards, mesh=mesh, in_specs=placed, out_specs=P(("groups", "blk", "pair")), check_vma=False
    )
```

```python
import functools

import jax
import jax.numpy as jnp
from jax import lax
from jax.experimental import pallas as pl
from jax.experimental.pallas import tpu as pltpu
from jax.sharding import PartitionSpec as P

SHARPNESS = 10.0
EPSILON = 1e-06
EMPTY_MARK = 2.0
EMPTY_ABOVE = 1.5
DIRECT_OWNERS = 8
SCORE_LANES = 128


def vmem(count):
    return [pl.BlockSpec(memory_space=pltpu.VMEM)] * count


def params(mib=24):
    return pltpu.CompilerParams(vmem_limit_bytes=mib * 1024 * 1024)


def prepare_kernel(owners, capacity, me_ref, rows_hbm, ids_hbm, *refs):
    block_refs = refs[:owners]
    pick_ref, rows_ref, ids_ref, sems = refs[owners:]
    ids_copy = pltpu.make_async_copy(ids_hbm, ids_ref, sems.at[0])
    rows_copy = pltpu.make_async_copy(rows_hbm, rows_ref, sems.at[1])
    ids_copy.start()
    rows_copy.start()
    row_count = ids_ref.shape[0]
    above = lax.broadcasted_iota(jnp.int32, (row_count, row_count), 0)
    right = lax.broadcasted_iota(jnp.int32, (row_count, row_count), 1)
    earlier = jnp.where(above < right, 1.0, 0.0).astype(jnp.bfloat16)
    labels = lax.broadcasted_iota(jnp.int32, (owners, row_count), 0)
    ids_copy.wait()
    step = jnp.reshape(ids_ref[...], (1, row_count)) ^ me_ref[0]
    relative = sum(jnp.where(step == value, k, 0) for k, value in enumerate(steps_of(owners)))
    inside = (labels == relative).astype(jnp.float32)
    before = jnp.dot(inside.astype(jnp.bfloat16), earlier, preferred_element_type=jnp.float32)
    rank = jnp.sum(before * inside, axis=0, keepdims=True).astype(jnp.int32)
    slot = relative * capacity + rank
    slots = owners * capacity
    pick_ref[...] = jnp.where(
        lax.broadcasted_iota(jnp.int32, (slots, row_count), 0) == slot, 1.0, 0.0
    ).astype(jnp.bfloat16)
    counts = jnp.broadcast_to(jnp.sum(inside, axis=1, keepdims=True), (owners, 128))
    first = lax.broadcasted_iota(jnp.int32, (owners, 128), 1) == 0
    marks = jnp.where(first & (counts == 0.0), EMPTY_MARK, 0.0)
    rows_copy.wait()
    values = rows_ref[...].astype(jnp.float32)
    scale = lax.rsqrt(jnp.sum(values * values, axis=1, keepdims=True) + EPSILON)
    units = (values * scale).astype(jnp.bfloat16)
    for k, block_ref in enumerate(block_refs):
        block = jnp.dot(
            pick_ref[k * capacity:(k + 1) * capacity, :], units, preferred_element_type=jnp.float32
        )
        block_ref[...] = block.astype(jnp.bfloat16)
        block_ref[:, 0:128] = (block[:, 0:128] + marks[k:k + 1, :]).astype(jnp.bfloat16)


def prepare(me, rows, ids, owners, capacity):
    row_count, width = rows.shape
    *blocks, pick = pl.pallas_call(
        functools.partial(prepare_kernel, owners, capacity),
        out_shape=[jax.ShapeDtypeStruct((capacity, width), jnp.bfloat16)] * owners
        + [jax.ShapeDtypeStruct((owners * capacity, row_count), jnp.bfloat16)],
        in_specs=[pl.BlockSpec(memory_space=pltpu.SMEM)] + [pl.BlockSpec(memory_space=pltpu.HBM)] * 2,
        out_specs=vmem(owners + 1),
        scratch_shapes=[
            pltpu.VMEM(rows.shape, rows.dtype),
            pltpu.VMEM(ids.shape, ids.dtype),
            pltpu.SemaphoreType.DMA((2,)),
        ],
        compiler_params=params(),
    )(
        me,
        pltpu.with_memory_space_constraint(rows, pltpu.HBM),
        pltpu.with_memory_space_constraint(ids, pltpu.HBM),
    )
    return blocks, pick


def partial_sums(own, others, others_refs, own_block):
    capacity = others_refs[0].shape[0]
    count = own.shape[0]
    total = jnp.zeros((1, count), jnp.float32)
    products = lax.dot_general(others, own, (((1,), (1,)), ((), ())), preferred_element_type=jnp.float32)
    for k, block_ref in enumerate(others_refs):
        powers = jnp.exp(products[k * capacity:(k + 1) * capacity] * SHARPNESS)
        if own_block:
            row = lax.broadcasted_iota(jnp.int32, powers.shape, 0) + k * capacity
            powers = jnp.where(row == lax.broadcasted_iota(jnp.int32, powers.shape, 1), 0.0, powers)
        living = block_ref[0:1, 0:1].astype(jnp.float32) < EMPTY_ABOVE
        total = total + jnp.where(living, jnp.sum(powers, axis=0, keepdims=True), 0.0)
    return total


def own_kernel(owners, *refs):
    block_refs, joined_ref, total_ref = refs[:owners], refs[owners], refs[owners + 1]
    capacity = block_refs[0].shape[0]
    for k, block_ref in enumerate(block_refs):
        joined_ref[k * capacity:(k + 1) * capacity, :] = block_ref[...]
    own = joined_ref[...]
    total_ref[...] = partial_sums(own, own, block_refs, True)


def own_sums(blocks):
    capacity, width = blocks[0].shape
    slots = len(blocks) * capacity
    return pl.pallas_call(
        functools.partial(own_kernel, len(blocks)),
        out_shape=[
            jax.ShapeDtypeStruct((slots, width), jnp.bfloat16),
            jax.ShapeDtypeStruct((1, slots), jnp.float32),
        ],
        in_specs=vmem(len(blocks)),
        out_specs=vmem(2),
        compiler_params=params(),
        cost_estimate=pl.CostEstimate(
            flops=2 * slots * slots * width, bytes_accessed=4 * slots * width, transcendentals=slots * slots
        ),
    )(*blocks)


def cross_kernel(owners, me_ref, *refs):
    block_refs, joined_ref, total_ref, score_ref, others_ref = refs[:owners], *refs[owners:]
    me = me_ref[0]
    capacity = block_refs[0].shape[0]
    for k, block_ref in enumerate(block_refs):
        others_ref[k * capacity:(k + 1) * capacity, :] = block_ref[...]
    total = total_ref[...] + partial_sums(joined_ref[...], others_ref[...], block_refs, False)
    scores = jnp.log(jnp.where(total > 0.0, total, 1.0))
    for k, step in enumerate(steps_of(owners)):
        score_ref[pl.ds(me ^ step, 1), 0:capacity] = scores[:, k * capacity:(k + 1) * capacity]


def cross_scores(me, blocks, joined, total):
    capacity, width = blocks[0].shape
    slots = len(blocks) * capacity
    return pl.pallas_call(
        functools.partial(cross_kernel, len(blocks)),
        out_shape=jax.ShapeDtypeStruct((len(blocks), SCORE_LANES), jnp.float32),
        in_specs=[pl.BlockSpec(memory_space=pltpu.SMEM)] + vmem(len(blocks) + 2),
        out_specs=pl.BlockSpec(memory_space=pltpu.VMEM),
        scratch_shapes=[pltpu.VMEM((slots, width), jnp.bfloat16)],
        compiler_params=params(),
    )(me, *blocks, joined, total)


def collect_kernel(capacity, me_ref, score_ref, pick_ref, out_ref):
    me = me_ref[0]
    scores = jnp.concatenate(
        [score_ref[pl.ds(me ^ step, 1), 0:capacity] for step in steps_of(score_ref.shape[0])], axis=1
    )
    high = scores.astype(jnp.bfloat16)
    rest = scores - high.astype(jnp.float32)
    middle = rest.astype(jnp.bfloat16)
    low = (rest - middle.astype(jnp.float32)).astype(jnp.bfloat16)
    parts = jnp.dot(
        jnp.concatenate([high, middle, low], axis=0), pick_ref[...], preferred_element_type=jnp.float32
    )
    out_ref[...] = jnp.reshape((parts[0:1] + parts[1:2]) + parts[2:3], out_ref.shape)


def collect(me, scores, pick, capacity):
    return pl.pallas_call(
        functools.partial(collect_kernel, capacity),
        out_shape=jax.ShapeDtypeStruct((pick.shape[1],), jnp.float32),
        in_specs=[pl.BlockSpec(memory_space=pltpu.SMEM)] + vmem(2),
        out_specs=pl.BlockSpec(memory_space=pltpu.VMEM),
        compiler_params=params(),
    )(me, scores, pick)


def steps_of(owners):
    if owners == 8:
        return (0, 6, 5, 3, 7, 1, 2, 4)
    return tuple(range(owners))


def swap(block, axis, step, size):
    if step == 0:
        return block
    return lax.ppermute(block, axis, [(i, i ^ step) for i in range(size)])


def direct_shards(embeddings, cluster_ids):
    owners = lax.axis_size("blk")
    capacity = 2 * embeddings.shape[0] // owners
    me = jnp.reshape(lax.axis_index("blk").astype(jnp.int32), (1,))
    blocks, pick = prepare(me, embeddings, cluster_ids, owners, capacity)
    own_blocks = [None] * owners
    for k, step in enumerate(steps_of(owners)):
        own_blocks[k] = swap(blocks[k], "blk", step, owners)
    other_blocks = [swap(block, "pair", 1, 2) for block in own_blocks]
    joined, total = own_sums(own_blocks)
    scores = cross_scores(me, other_blocks, joined, total)
    returned = lax.all_to_all(scores, "blk", split_axis=0, concat_axis=0, tiled=True)
    return collect(me, returned, pick, capacity)


def unit_vectors(values):
    widened = values.astype(jnp.float32)
    scale = lax.rsqrt(jnp.sum(widened * widened, axis=1, keepdims=True) + EPSILON)
    return (widened * scale).astype(jnp.bfloat16)


def wide_shards(embeddings, cluster_ids):
    row_count, width = embeddings.shape
    owners = lax.axis_size("blk")
    capacity = 2 * row_count // owners
    slots = owners * capacity
    units = unit_vectors(embeddings)
    marks = (cluster_ids[:, None] == jnp.arange(owners, dtype=jnp.int32)[None, :]).astype(jnp.bfloat16)
    row_order = jnp.arange(row_count, dtype=jnp.int32)
    earlier = (row_order[:, None] > row_order[None, :]).astype(jnp.bfloat16)
    before = jnp.dot(earlier, marks, preferred_element_type=jnp.float32)
    rank = jnp.sum(before * marks.astype(jnp.float32), axis=1).astype(jnp.int32)
    target = cluster_ids * capacity + rank
    empty_row = jnp.where(jnp.arange(width) == 0, EMPTY_MARK, 0.0).astype(jnp.bfloat16)
    send = jnp.broadcast_to(empty_row[None, :], (slots, width)).at[target].set(units)
    own = lax.all_to_all(
        send.reshape(owners, capacity, width), "blk", split_axis=0, concat_axis=0, tiled=True
    ).reshape(slots, width)
    other = lax.ppermute(own, "pair", [(0, 1), (1, 0)])
    columns = jnp.concatenate([own, other], axis=0)
    living = columns[:, 0].astype(jnp.float32) < EMPTY_ABOVE
    products = lax.dot_general(own, columns, (((1,), (1,)), ((), ())), preferred_element_type=jnp.float32)
    position = jnp.arange(2 * slots, dtype=jnp.int32)
    keep = living[None, :] & (position[:slots, None] != position[None, :])
    density = jnp.sum(jnp.where(keep, jnp.exp(products * SHARPNESS), 0.0), axis=1)
    scores = jnp.log(jnp.where(living[:slots], density, 1.0)).reshape(owners, capacity)
    returned = lax.all_to_all(scores, "blk", split_axis=0, concat_axis=0, tiled=True)
    return returned.reshape(slots)[target]


def solution(mesh):
    placed = (P(("groups", "blk", "pair"), None), P(("groups", "blk", "pair")))
    shards = direct_shards if mesh.shape["blk"] <= DIRECT_OWNERS else wide_shards
    return jax.shard_map(
        shards, mesh=mesh, in_specs=placed, out_specs=P(("groups", "blk", "pair")), check_vma=False
    )
```

```python
import functools

import jax
import jax.numpy as jnp
from jax import lax
from jax.experimental import pallas as pl
from jax.experimental.pallas import tpu as pltpu
from jax.sharding import PartitionSpec as P

SHARPNESS = 10.0
EPSILON = 1e-06
EMPTY_MARK = 2.0
EMPTY_ABOVE = 1.5
DIRECT_OWNERS = 8
SCORE_LANES = 128
COLUMNS = 256


def vmem(count):
    return [pl.BlockSpec(memory_space=pltpu.VMEM)] * count


def params(mib=24):
    return pltpu.CompilerParams(vmem_limit_bytes=mib * 1024 * 1024)


def prepare_kernel(owners, capacity, me_ref, rows_hbm, ids_hbm, *refs):
    block_refs = refs[:owners]
    pick_ref, rows_ref, ids_ref, sems = refs[owners:]
    ids_copy = pltpu.make_async_copy(ids_hbm, ids_ref, sems.at[0])
    rows_copy = pltpu.make_async_copy(rows_hbm, rows_ref, sems.at[1])
    ids_copy.start()
    rows_copy.start()
    row_count = ids_ref.shape[0]
    above = lax.broadcasted_iota(jnp.int32, (row_count, row_count), 0)
    right = lax.broadcasted_iota(jnp.int32, (row_count, row_count), 1)
    earlier = jnp.where(above < right, 1.0, 0.0).astype(jnp.bfloat16)
    labels = lax.broadcasted_iota(jnp.int32, (owners, row_count), 0)
    ids_copy.wait()
    step = jnp.reshape(ids_ref[...], (1, row_count)) ^ me_ref[0]
    relative = sum(jnp.where(step == value, k, 0) for k, value in enumerate(steps_of(owners)))
    inside = (labels == relative).astype(jnp.float32)
    before = jnp.dot(inside.astype(jnp.bfloat16), earlier, preferred_element_type=jnp.float32)
    rank = jnp.sum(before * inside, axis=0, keepdims=True).astype(jnp.int32)
    slot = relative * capacity + rank
    slots = owners * capacity
    pick_ref[...] = jnp.where(
        lax.broadcasted_iota(jnp.int32, (slots, row_count), 0) == slot, 1.0, 0.0
    ).astype(jnp.bfloat16)
    counts = jnp.broadcast_to(jnp.sum(inside, axis=1, keepdims=True), (owners, 128))
    first = lax.broadcasted_iota(jnp.int32, (owners, 128), 1) == 0
    marks = jnp.where(first & (counts == 0.0), EMPTY_MARK, 0.0)
    rows_copy.wait()
    values = rows_ref[...].astype(jnp.float32)
    scale = lax.rsqrt(jnp.sum(values * values, axis=1, keepdims=True) + EPSILON)
    units = (values * scale).astype(jnp.bfloat16)
    width = units.shape[1]
    for left in range(0, width, COLUMNS):
        right = min(left + COLUMNS, width)
        columns = jnp.dot(pick_ref[...], units[:, left:right], preferred_element_type=jnp.float32)
        for k, block_ref in enumerate(block_refs):
            block = columns[k * capacity:(k + 1) * capacity]
            if left == 0:
                block_ref[:, 0:128] = (block[:, 0:128] + marks[k:k + 1, :]).astype(jnp.bfloat16)
                block_ref[:, 128:right] = block[:, 128:].astype(jnp.bfloat16)
            else:
                block_ref[:, left:right] = block.astype(jnp.bfloat16)


def prepare(me, rows, ids, owners, capacity):
    row_count, width = rows.shape
    *blocks, pick = pl.pallas_call(
        functools.partial(prepare_kernel, owners, capacity),
        out_shape=[jax.ShapeDtypeStruct((capacity, width), jnp.bfloat16)] * owners
        + [jax.ShapeDtypeStruct((owners * capacity, row_count), jnp.bfloat16)],
        in_specs=[pl.BlockSpec(memory_space=pltpu.SMEM)] + [pl.BlockSpec(memory_space=pltpu.HBM)] * 2,
        out_specs=vmem(owners + 1),
        scratch_shapes=[
            pltpu.VMEM(rows.shape, rows.dtype),
            pltpu.VMEM(ids.shape, ids.dtype),
            pltpu.SemaphoreType.DMA((2,)),
        ],
        compiler_params=params(),
    )(
        me,
        pltpu.with_memory_space_constraint(rows, pltpu.HBM),
        pltpu.with_memory_space_constraint(ids, pltpu.HBM),
    )
    return blocks, pick


def partial_sums(own, others, others_refs, own_block):
    capacity = others_refs[0].shape[0]
    count = own.shape[0]
    total = jnp.zeros((1, count), jnp.float32)
    products = lax.dot_general(others, own, (((1,), (1,)), ((), ())), preferred_element_type=jnp.float32)
    for k, block_ref in enumerate(others_refs):
        powers = jnp.exp(products[k * capacity:(k + 1) * capacity] * SHARPNESS)
        if own_block:
            row = lax.broadcasted_iota(jnp.int32, powers.shape, 0) + k * capacity
            powers = jnp.where(row == lax.broadcasted_iota(jnp.int32, powers.shape, 1), 0.0, powers)
        living = block_ref[0:1, 0:1].astype(jnp.float32) < EMPTY_ABOVE
        total = total + jnp.where(living, jnp.sum(powers, axis=0, keepdims=True), 0.0)
    return total


def own_kernel(owners, *refs):
    block_refs, joined_ref, total_ref = refs[:owners], refs[owners], refs[owners + 1]
    capacity = block_refs[0].shape[0]
    for k, block_ref in enumerate(block_refs):
        joined_ref[k * capacity:(k + 1) * capacity, :] = block_ref[...]
    own = joined_ref[...]
    total_ref[...] = partial_sums(own, own, block_refs, True)


def own_sums(blocks):
    capacity, width = blocks[0].shape
    slots = len(blocks) * capacity
    return pl.pallas_call(
        functools.partial(own_kernel, len(blocks)),
        out_shape=[
            jax.ShapeDtypeStruct((slots, width), jnp.bfloat16),
            jax.ShapeDtypeStruct((1, slots), jnp.float32),
        ],
        in_specs=vmem(len(blocks)),
        out_specs=vmem(2),
        compiler_params=params(),
        cost_estimate=pl.CostEstimate(
            flops=2 * slots * slots * width, bytes_accessed=4 * slots * width, transcendentals=slots * slots
        ),
    )(*blocks)


def cross_kernel(owners, me_ref, *refs):
    block_refs, joined_ref, total_ref, score_ref, others_ref = refs[:owners], *refs[owners:]
    me = me_ref[0]
    capacity = block_refs[0].shape[0]
    for k, block_ref in enumerate(block_refs):
        others_ref[k * capacity:(k + 1) * capacity, :] = block_ref[...]
    total = total_ref[...] + partial_sums(joined_ref[...], others_ref[...], block_refs, False)
    scores = jnp.log(jnp.where(total > 0.0, total, 1.0))
    for k, step in enumerate(steps_of(owners)):
        score_ref[pl.ds(me ^ step, 1), 0:capacity] = scores[:, k * capacity:(k + 1) * capacity]


def cross_scores(me, blocks, joined, total):
    capacity, width = blocks[0].shape
    slots = len(blocks) * capacity
    return pl.pallas_call(
        functools.partial(cross_kernel, len(blocks)),
        out_shape=jax.ShapeDtypeStruct((len(blocks), SCORE_LANES), jnp.float32),
        in_specs=[pl.BlockSpec(memory_space=pltpu.SMEM)] + vmem(len(blocks) + 2),
        out_specs=pl.BlockSpec(memory_space=pltpu.VMEM),
        scratch_shapes=[pltpu.VMEM((slots, width), jnp.bfloat16)],
        compiler_params=params(),
    )(me, *blocks, joined, total)


def collect_kernel(capacity, me_ref, score_ref, pick_ref, out_ref):
    me = me_ref[0]
    scores = jnp.concatenate(
        [score_ref[pl.ds(me ^ step, 1), 0:capacity] for step in steps_of(score_ref.shape[0])], axis=1
    )
    high = scores.astype(jnp.bfloat16)
    rest = scores - high.astype(jnp.float32)
    middle = rest.astype(jnp.bfloat16)
    low = (rest - middle.astype(jnp.float32)).astype(jnp.bfloat16)
    parts = jnp.dot(
        jnp.concatenate([high, middle, low], axis=0), pick_ref[...], preferred_element_type=jnp.float32
    )
    out_ref[...] = jnp.reshape((parts[0:1] + parts[1:2]) + parts[2:3], out_ref.shape)


def collect(me, scores, pick, capacity):
    return pl.pallas_call(
        functools.partial(collect_kernel, capacity),
        out_shape=jax.ShapeDtypeStruct((pick.shape[1],), jnp.float32),
        in_specs=[pl.BlockSpec(memory_space=pltpu.SMEM)] + vmem(2),
        out_specs=pl.BlockSpec(memory_space=pltpu.VMEM),
        compiler_params=params(),
    )(me, scores, pick)


def steps_of(owners):
    if owners == 8:
        return (0, 6, 5, 3, 7, 1, 2, 4)
    return tuple(range(owners))


def swap(block, axis, step, size):
    if step == 0:
        return block
    return lax.ppermute(block, axis, [(i, i ^ step) for i in range(size)])


def direct_shards(embeddings, cluster_ids):
    owners = lax.axis_size("blk")
    capacity = 2 * embeddings.shape[0] // owners
    me = jnp.reshape(lax.axis_index("blk").astype(jnp.int32), (1,))
    blocks, pick = prepare(me, embeddings, cluster_ids, owners, capacity)
    own_blocks = [None] * owners
    for k, step in enumerate(steps_of(owners)):
        own_blocks[k] = swap(blocks[k], "blk", step, owners)
    other_blocks = [swap(block, "pair", 1, 2) for block in own_blocks]
    joined, total = own_sums(own_blocks)
    scores = cross_scores(me, other_blocks, joined, total)
    returned = lax.all_to_all(scores, "blk", split_axis=0, concat_axis=0, tiled=True)
    return collect(me, returned, pick, capacity)


def unit_vectors(values):
    widened = values.astype(jnp.float32)
    scale = lax.rsqrt(jnp.sum(widened * widened, axis=1, keepdims=True) + EPSILON)
    return (widened * scale).astype(jnp.bfloat16)


def wide_shards(embeddings, cluster_ids):
    row_count, width = embeddings.shape
    owners = lax.axis_size("blk")
    capacity = 2 * row_count // owners
    slots = owners * capacity
    units = unit_vectors(embeddings)
    marks = (cluster_ids[:, None] == jnp.arange(owners, dtype=jnp.int32)[None, :]).astype(jnp.bfloat16)
    row_order = jnp.arange(row_count, dtype=jnp.int32)
    earlier = (row_order[:, None] > row_order[None, :]).astype(jnp.bfloat16)
    before = jnp.dot(earlier, marks, preferred_element_type=jnp.float32)
    rank = jnp.sum(before * marks.astype(jnp.float32), axis=1).astype(jnp.int32)
    target = cluster_ids * capacity + rank
    empty_row = jnp.where(jnp.arange(width) == 0, EMPTY_MARK, 0.0).astype(jnp.bfloat16)
    send = jnp.broadcast_to(empty_row[None, :], (slots, width)).at[target].set(units)
    own = lax.all_to_all(
        send.reshape(owners, capacity, width), "blk", split_axis=0, concat_axis=0, tiled=True
    ).reshape(slots, width)
    other = lax.ppermute(own, "pair", [(0, 1), (1, 0)])
    columns = jnp.concatenate([own, other], axis=0)
    living = columns[:, 0].astype(jnp.float32) < EMPTY_ABOVE
    products = lax.dot_general(own, columns, (((1,), (1,)), ((), ())), preferred_element_type=jnp.float32)
    position = jnp.arange(2 * slots, dtype=jnp.int32)
    keep = living[None, :] & (position[:slots, None] != position[None, :])
    density = jnp.sum(jnp.where(keep, jnp.exp(products * SHARPNESS), 0.0), axis=1)
    scores = jnp.log(jnp.where(living[:slots], density, 1.0)).reshape(owners, capacity)
    returned = lax.all_to_all(scores, "blk", split_axis=0, concat_axis=0, tiled=True)
    return returned.reshape(slots)[target]


def solution(mesh):
    placed = (P(("groups", "blk", "pair"), None), P(("groups", "blk", "pair")))
    shards = direct_shards if mesh.shape["blk"] <= DIRECT_OWNERS else wide_shards
    return jax.shard_map(
        shards, mesh=mesh, in_specs=placed, out_specs=P(("groups", "blk", "pair")), check_vma=False
    )
```

```python
import functools
import math

import jax
import jax.numpy as jnp
from jax import lax
from jax.experimental import pallas as pl
from jax.experimental.pallas import tpu as pltpu
from jax.sharding import PartitionSpec as P

SHARPNESS = 10.0
SHARPNESS_LOG2 = SHARPNESS * math.log2(math.e)
EPSILON = 1e-06
EMPTY_MARK = 2.0
EMPTY_ABOVE = 1.5
DIRECT_OWNERS = 8
SCORE_LANES = 128
COLUMNS = 256


def vmem(count):
    return [pl.BlockSpec(memory_space=pltpu.VMEM)] * count


def params(mib=24):
    return pltpu.CompilerParams(vmem_limit_bytes=mib * 1024 * 1024)


def prepare_kernel(owners, capacity, me_ref, rows_hbm, ids_hbm, *refs):
    block_refs = refs[:owners]
    ranks_ref, ids_row_ref, pick_ref, rows_ref, ids_ref, sems = refs[owners:]
    ids_copy = pltpu.make_async_copy(ids_hbm, ids_ref, sems.at[0])
    rows_copy = pltpu.make_async_copy(rows_hbm, rows_ref, sems.at[1])
    ids_copy.start()
    rows_copy.start()
    row_count = ids_ref.shape[0]
    above = lax.broadcasted_iota(jnp.int32, (row_count, row_count), 0)
    right = lax.broadcasted_iota(jnp.int32, (row_count, row_count), 1)
    earlier = jnp.where(above < right, 1.0, 0.0).astype(jnp.bfloat16)
    labels = lax.broadcasted_iota(jnp.int32, (owners, row_count), 0)
    ids_copy.wait()
    ids = jnp.reshape(ids_ref[...], (1, row_count))
    ids_row_ref[...] = ids
    step = ids ^ me_ref[0]
    relative = sum(jnp.where(step == value, k, 0) for k, value in enumerate(steps_of(owners)))
    inside = (labels == relative).astype(jnp.float32)
    before = jnp.dot(inside.astype(jnp.bfloat16), earlier, preferred_element_type=jnp.float32)
    rank = jnp.sum(before * inside, axis=0, keepdims=True).astype(jnp.int32)
    slot = relative * capacity + rank
    slots = owners * capacity
    pick_ref[...] = jnp.where(
        lax.broadcasted_iota(jnp.int32, (slots, row_count), 0) == slot, 1.0, 0.0
    ).astype(jnp.bfloat16)
    ranks_ref[...] = jnp.where(
        lax.broadcasted_iota(jnp.int32, (capacity, row_count), 0) == rank, 1.0, 0.0
    ).astype(jnp.bfloat16)
    counts = jnp.broadcast_to(jnp.sum(inside, axis=1, keepdims=True), (owners, 128))
    first = lax.broadcasted_iota(jnp.int32, (owners, 128), 1) == 0
    marks = jnp.where(first & (counts == 0.0), EMPTY_MARK, 0.0)
    rows_copy.wait()
    values = rows_ref[...].astype(jnp.float32)
    scale = lax.rsqrt(jnp.sum(values * values, axis=1, keepdims=True) + EPSILON)
    units = (values * scale).astype(jnp.bfloat16)
    width = units.shape[1]
    for left in range(0, width, COLUMNS):
        right = min(left + COLUMNS, width)
        columns = jnp.dot(pick_ref[...], units[:, left:right], preferred_element_type=jnp.float32)
        for k, block_ref in enumerate(block_refs):
            block = columns[k * capacity:(k + 1) * capacity]
            if left == 0:
                block_ref[:, 0:128] = (block[:, 0:128] + marks[k:k + 1, :]).astype(jnp.bfloat16)
                block_ref[:, 128:right] = block[:, 128:].astype(jnp.bfloat16)
            else:
                block_ref[:, left:right] = block.astype(jnp.bfloat16)


def prepare(me, rows, ids, owners, capacity):
    row_count, width = rows.shape
    *blocks, ranks, ids_row = pl.pallas_call(
        functools.partial(prepare_kernel, owners, capacity),
        out_shape=[jax.ShapeDtypeStruct((capacity, width), jnp.bfloat16)] * owners
        + [
            jax.ShapeDtypeStruct((capacity, row_count), jnp.bfloat16),
            jax.ShapeDtypeStruct((1, row_count), jnp.int32),
        ],
        in_specs=[pl.BlockSpec(memory_space=pltpu.SMEM)] + [pl.BlockSpec(memory_space=pltpu.HBM)] * 2,
        out_specs=vmem(owners + 2),
        scratch_shapes=[
            pltpu.VMEM((owners * capacity, row_count), jnp.bfloat16),
            pltpu.VMEM(rows.shape, rows.dtype),
            pltpu.VMEM(ids.shape, ids.dtype),
            pltpu.SemaphoreType.DMA((2,)),
        ],
        compiler_params=params(),
    )(
        me,
        pltpu.with_memory_space_constraint(rows, pltpu.HBM),
        pltpu.with_memory_space_constraint(ids, pltpu.HBM),
    )
    return blocks, ranks, ids_row


def partial_sums(own, others, others_refs, own_block):
    capacity = others_refs[0].shape[0]
    count = own.shape[0]
    total = jnp.zeros((1, count), jnp.float32)
    products = lax.dot_general(others, own, (((1,), (1,)), ((), ())), preferred_element_type=jnp.float32)
    for k, block_ref in enumerate(others_refs):
        powers = jnp.exp2(products[k * capacity:(k + 1) * capacity] * SHARPNESS_LOG2)
        if own_block:
            row = lax.broadcasted_iota(jnp.int32, powers.shape, 0) + k * capacity
            powers = jnp.where(row == lax.broadcasted_iota(jnp.int32, powers.shape, 1), 0.0, powers)
        living = block_ref[0:1, 0:1].astype(jnp.float32) < EMPTY_ABOVE
        total = total + jnp.where(living, jnp.sum(powers, axis=0, keepdims=True), 0.0)
    return total


def own_kernel(owners, *refs):
    block_refs, joined_ref, total_ref = refs[:owners], refs[owners], refs[owners + 1]
    capacity = block_refs[0].shape[0]
    for k, block_ref in enumerate(block_refs):
        joined_ref[k * capacity:(k + 1) * capacity, :] = block_ref[...]
    own = joined_ref[...]
    total_ref[...] = partial_sums(own, own, block_refs, True)


def own_sums(blocks):
    capacity, width = blocks[0].shape
    slots = len(blocks) * capacity
    return pl.pallas_call(
        functools.partial(own_kernel, len(blocks)),
        out_shape=[
            jax.ShapeDtypeStruct((slots, width), jnp.bfloat16),
            jax.ShapeDtypeStruct((1, slots), jnp.float32),
        ],
        in_specs=vmem(len(blocks)),
        out_specs=vmem(2),
        compiler_params=params(),
        cost_estimate=pl.CostEstimate(
            flops=2 * slots * slots * width, bytes_accessed=4 * slots * width, transcendentals=slots * slots
        ),
    )(*blocks)


def cross_kernel(owners, me_ref, *refs):
    block_refs, joined_ref, total_ref, score_ref, others_ref = refs[:owners], *refs[owners:]
    me = me_ref[0]
    capacity = block_refs[0].shape[0]
    for k, block_ref in enumerate(block_refs):
        others_ref[k * capacity:(k + 1) * capacity, :] = block_ref[...]
    total = total_ref[...] + partial_sums(joined_ref[...], others_ref[...], block_refs, False)
    scores = jnp.log(jnp.where(total > 0.0, total, 1.0))
    for k, step in enumerate(steps_of(owners)):
        score_ref[pl.ds(me ^ step, 1), 0:capacity] = scores[:, k * capacity:(k + 1) * capacity]


def cross_scores(me, blocks, joined, total):
    capacity, width = blocks[0].shape
    slots = len(blocks) * capacity
    return pl.pallas_call(
        functools.partial(cross_kernel, len(blocks)),
        out_shape=jax.ShapeDtypeStruct((len(blocks), SCORE_LANES), jnp.float32),
        in_specs=[pl.BlockSpec(memory_space=pltpu.SMEM)] + vmem(len(blocks) + 2),
        out_specs=pl.BlockSpec(memory_space=pltpu.VMEM),
        scratch_shapes=[pltpu.VMEM((slots, width), jnp.bfloat16)],
        compiler_params=params(),
    )(me, *blocks, joined, total)


def collect_kernel(score_ref, ranks_ref, ids_ref, out_ref):
    owners = score_ref.shape[0]
    capacity, row_count = ranks_ref.shape
    scores = score_ref[:, 0:capacity]
    high = scores.astype(jnp.bfloat16)
    rest = scores - high.astype(jnp.float32)
    middle = rest.astype(jnp.bfloat16)
    low = (rest - middle.astype(jnp.float32)).astype(jnp.bfloat16)
    ranks = ranks_ref[...]
    by_rank = (
        jnp.dot(high, ranks, preferred_element_type=jnp.float32)
        + jnp.dot(middle, ranks, preferred_element_type=jnp.float32)
    ) + jnp.dot(low, ranks, preferred_element_type=jnp.float32)
    own = lax.broadcasted_iota(jnp.int32, (owners, row_count), 0) == ids_ref[...]
    out_ref[...] = jnp.reshape(jnp.sum(jnp.where(own, by_rank, 0.0), axis=0, keepdims=True), out_ref.shape)


def collect(scores, ranks, ids):
    return pl.pallas_call(
        collect_kernel,
        out_shape=jax.ShapeDtypeStruct((ranks.shape[1],), jnp.float32),
        in_specs=vmem(3),
        out_specs=pl.BlockSpec(memory_space=pltpu.VMEM),
        compiler_params=params(),
    )(scores, ranks, ids)


def steps_of(owners):
    if owners == 8:
        return (0, 6, 5, 3, 7, 1, 2, 4)
    return tuple(range(owners))


def swap(block, axis, step, size):
    if step == 0:
        return block
    return lax.ppermute(block, axis, [(i, i ^ step) for i in range(size)])


def direct_shards(embeddings, cluster_ids):
    owners = lax.axis_size("blk")
    capacity = 2 * embeddings.shape[0] // owners
    me = jnp.reshape(lax.axis_index("blk").astype(jnp.int32), (1,))
    blocks, ranks, ids = prepare(me, embeddings, cluster_ids, owners, capacity)
    own_blocks = [None] * owners
    for k, step in enumerate(steps_of(owners)):
        own_blocks[k] = swap(blocks[k], "blk", step, owners)
    other_blocks = [swap(block, "pair", 1, 2) for block in own_blocks]
    joined, total = own_sums(own_blocks)
    scores = cross_scores(me, other_blocks, joined, total)
    returned = lax.all_to_all(scores, "blk", split_axis=0, concat_axis=0, tiled=True)
    return collect(returned, ranks, ids)


def unit_vectors(values):
    widened = values.astype(jnp.float32)
    scale = lax.rsqrt(jnp.sum(widened * widened, axis=1, keepdims=True) + EPSILON)
    return (widened * scale).astype(jnp.bfloat16)


def wide_shards(embeddings, cluster_ids):
    row_count, width = embeddings.shape
    owners = lax.axis_size("blk")
    capacity = 2 * row_count // owners
    slots = owners * capacity
    units = unit_vectors(embeddings)
    marks = (cluster_ids[:, None] == jnp.arange(owners, dtype=jnp.int32)[None, :]).astype(jnp.bfloat16)
    row_order = jnp.arange(row_count, dtype=jnp.int32)
    earlier = (row_order[:, None] > row_order[None, :]).astype(jnp.bfloat16)
    before = jnp.dot(earlier, marks, preferred_element_type=jnp.float32)
    rank = jnp.sum(before * marks.astype(jnp.float32), axis=1).astype(jnp.int32)
    target = cluster_ids * capacity + rank
    empty_row = jnp.where(jnp.arange(width) == 0, EMPTY_MARK, 0.0).astype(jnp.bfloat16)
    send = jnp.broadcast_to(empty_row[None, :], (slots, width)).at[target].set(units)
    own = lax.all_to_all(
        send.reshape(owners, capacity, width), "blk", split_axis=0, concat_axis=0, tiled=True
    ).reshape(slots, width)
    other = lax.ppermute(own, "pair", [(0, 1), (1, 0)])
    columns = jnp.concatenate([own, other], axis=0)
    living = columns[:, 0].astype(jnp.float32) < EMPTY_ABOVE
    products = lax.dot_general(own, columns, (((1,), (1,)), ((), ())), preferred_element_type=jnp.float32)
    position = jnp.arange(2 * slots, dtype=jnp.int32)
    keep = living[None, :] & (position[:slots, None] != position[None, :])
    density = jnp.sum(jnp.where(keep, jnp.exp(products * SHARPNESS), 0.0), axis=1)
    scores = jnp.log(jnp.where(living[:slots], density, 1.0)).reshape(owners, capacity)
    returned = lax.all_to_all(scores, "blk", split_axis=0, concat_axis=0, tiled=True)
    return returned.reshape(slots)[target]


def solution(mesh):
    placed = (P(("groups", "blk", "pair"), None), P(("groups", "blk", "pair")))
    shards = direct_shards if mesh.shape["blk"] <= DIRECT_OWNERS else wide_shards
    return jax.shard_map(
        shards, mesh=mesh, in_specs=placed, out_specs=P(("groups", "blk", "pair")), check_vma=False
    )
```

```python
import functools
import math

import jax
import jax.numpy as jnp
from jax import lax
from jax.experimental import pallas as pl
from jax.experimental.pallas import tpu as pltpu
from jax.sharding import PartitionSpec as P

SHARPNESS = 10.0
SHARPNESS_LOG2 = SHARPNESS * math.log2(math.e)
EPSILON = 1e-06
EMPTY_MARK = 2.0
EMPTY_ABOVE = 1.5
DIRECT_OWNERS = 8
SCORE_LANES = 128
COLUMNS = 256


def vmem(count):
    return [pl.BlockSpec(memory_space=pltpu.VMEM)] * count


def params(mib=24):
    return pltpu.CompilerParams(vmem_limit_bytes=mib * 1024 * 1024)


def prepare_kernel(owners, capacity, me_ref, rows_hbm, ids_hbm, *refs):
    block_refs = refs[:owners]
    ranks_ref, ids_row_ref, pick_ref, rows_ref, ids_ref, sems = refs[owners:]
    ids_copy = pltpu.make_async_copy(ids_hbm, ids_ref, sems.at[0])
    rows_copy = pltpu.make_async_copy(rows_hbm, rows_ref, sems.at[1])
    ids_copy.start()
    rows_copy.start()
    row_count = ids_ref.shape[0]
    above = lax.broadcasted_iota(jnp.int32, (row_count, row_count), 0)
    right = lax.broadcasted_iota(jnp.int32, (row_count, row_count), 1)
    earlier = jnp.where(above < right, 1.0, 0.0).astype(jnp.bfloat16)
    labels = lax.broadcasted_iota(jnp.int32, (owners, row_count), 0)
    ids_copy.wait()
    ids = jnp.reshape(ids_ref[...], (1, row_count))
    ids_row_ref[...] = ids
    step = ids ^ me_ref[0]
    relative = sum(jnp.where(step == value, k, 0) for k, value in enumerate(steps_of(owners)))
    inside = (labels == relative).astype(jnp.float32)
    before = jnp.dot(inside.astype(jnp.bfloat16), earlier, preferred_element_type=jnp.float32)
    rank = jnp.sum(before * inside, axis=0, keepdims=True).astype(jnp.int32)
    slot = relative * capacity + rank
    slots = owners * capacity
    pick_ref[...] = jnp.where(
        lax.broadcasted_iota(jnp.int32, (slots, row_count), 0) == slot, 1.0, 0.0
    ).astype(jnp.bfloat16)
    ranks_ref[...] = jnp.where(
        lax.broadcasted_iota(jnp.int32, (capacity, row_count), 0) == rank, 1.0, 0.0
    ).astype(jnp.bfloat16)
    counts = jnp.broadcast_to(jnp.sum(inside, axis=1, keepdims=True), (owners, 128))
    first = lax.broadcasted_iota(jnp.int32, (owners, 128), 1) == 0
    marks = jnp.where(first & (counts == 0.0), EMPTY_MARK, 0.0)
    rows_copy.wait()
    values = rows_ref[...].astype(jnp.float32)
    scale = lax.rsqrt(jnp.sum(values * values, axis=1, keepdims=True) + EPSILON)
    units = (values * scale).astype(jnp.bfloat16)
    width = units.shape[1]
    for left in range(0, width, COLUMNS):
        right = min(left + COLUMNS, width)
        columns = jnp.dot(pick_ref[...], units[:, left:right], preferred_element_type=jnp.float32)
        for k, block_ref in enumerate(block_refs):
            block = columns[k * capacity:(k + 1) * capacity]
            if left == 0:
                block_ref[:, 0:128] = (block[:, 0:128] + marks[k:k + 1, :]).astype(jnp.bfloat16)
                block_ref[:, 128:right] = block[:, 128:].astype(jnp.bfloat16)
            else:
                block_ref[:, left:right] = block.astype(jnp.bfloat16)


def prepare(me, rows, ids, owners, capacity):
    row_count, width = rows.shape
    *blocks, ranks, ids_row = pl.pallas_call(
        functools.partial(prepare_kernel, owners, capacity),
        out_shape=[jax.ShapeDtypeStruct((capacity, width), jnp.bfloat16)] * owners
        + [
            jax.ShapeDtypeStruct((capacity, row_count), jnp.bfloat16),
            jax.ShapeDtypeStruct((1, row_count), jnp.int32),
        ],
        in_specs=[pl.BlockSpec(memory_space=pltpu.SMEM)] + [pl.BlockSpec(memory_space=pltpu.HBM)] * 2,
        out_specs=vmem(owners + 2),
        scratch_shapes=[
            pltpu.VMEM((owners * capacity, row_count), jnp.bfloat16),
            pltpu.VMEM(rows.shape, rows.dtype),
            pltpu.VMEM(ids.shape, ids.dtype),
            pltpu.SemaphoreType.DMA((2,)),
        ],
        compiler_params=params(),
    )(
        me,
        pltpu.with_memory_space_constraint(rows, pltpu.HBM),
        pltpu.with_memory_space_constraint(ids, pltpu.HBM),
    )
    return blocks, ranks, ids_row


def partial_sums(own, others, others_refs, own_block):
    capacity = others_refs[0].shape[0]
    count = own.shape[0]
    total = jnp.zeros((1, count), jnp.float32)
    products = lax.dot_general(others, own, (((1,), (1,)), ((), ())), preferred_element_type=jnp.float32)
    for k, block_ref in enumerate(others_refs):
        powers = jnp.exp2(products[k * capacity:(k + 1) * capacity] * SHARPNESS_LOG2)
        if own_block:
            row = lax.broadcasted_iota(jnp.int32, powers.shape, 0) + k * capacity
            powers = jnp.where(row == lax.broadcasted_iota(jnp.int32, powers.shape, 1), 0.0, powers)
        living = block_ref[0:16, 0:128].astype(jnp.float32)[0:1, 0:1] < EMPTY_ABOVE
        total = total + jnp.where(living, jnp.sum(powers, axis=0, keepdims=True), 0.0)
    return total


def own_kernel(owners, *refs):
    block_refs, joined_ref, total_ref = refs[:owners], refs[owners], refs[owners + 1]
    capacity = block_refs[0].shape[0]
    for k, block_ref in enumerate(block_refs):
        joined_ref[k * capacity:(k + 1) * capacity, :] = block_ref[...]
    own = joined_ref[...]
    total_ref[...] = partial_sums(own, own, block_refs, True)


def own_sums(blocks):
    capacity, width = blocks[0].shape
    slots = len(blocks) * capacity
    return pl.pallas_call(
        functools.partial(own_kernel, len(blocks)),
        out_shape=[
            jax.ShapeDtypeStruct((slots, width), jnp.bfloat16),
            jax.ShapeDtypeStruct((1, slots), jnp.float32),
        ],
        in_specs=vmem(len(blocks)),
        out_specs=vmem(2),
        compiler_params=params(),
        cost_estimate=pl.CostEstimate(
            flops=2 * slots * slots * width, bytes_accessed=4 * slots * width, transcendentals=slots * slots
        ),
    )(*blocks)


def cross_kernel(owners, me_ref, *refs):
    block_refs, joined_ref, total_ref, score_ref, others_ref = refs[:owners], *refs[owners:]
    me = me_ref[0]
    capacity = block_refs[0].shape[0]
    for k, block_ref in enumerate(block_refs):
        others_ref[k * capacity:(k + 1) * capacity, :] = block_ref[...]
    total = total_ref[...] + partial_sums(joined_ref[...], others_ref[...], block_refs, False)
    scores = jnp.log(jnp.where(total > 0.0, total, 1.0))
    for k, step in enumerate(steps_of(owners)):
        score_ref[pl.ds(me ^ step, 1), 0:capacity] = scores[:, k * capacity:(k + 1) * capacity]


def cross_scores(me, blocks, joined, total):
    capacity, width = blocks[0].shape
    slots = len(blocks) * capacity
    return pl.pallas_call(
        functools.partial(cross_kernel, len(blocks)),
        out_shape=jax.ShapeDtypeStruct((len(blocks), SCORE_LANES), jnp.float32),
        in_specs=[pl.BlockSpec(memory_space=pltpu.SMEM)] + vmem(len(blocks) + 2),
        out_specs=pl.BlockSpec(memory_space=pltpu.VMEM),
        scratch_shapes=[pltpu.VMEM((slots, width), jnp.bfloat16)],
        compiler_params=params(),
    )(me, *blocks, joined, total)


def collect_kernel(score_ref, ranks_ref, ids_ref, out_ref):
    owners = score_ref.shape[0]
    capacity, row_count = ranks_ref.shape
    scores = score_ref[:, 0:capacity]
    high = scores.astype(jnp.bfloat16)
    rest = scores - high.astype(jnp.float32)
    middle = rest.astype(jnp.bfloat16)
    low = (rest - middle.astype(jnp.float32)).astype(jnp.bfloat16)
    ranks = ranks_ref[...]
    by_rank = (
        jnp.dot(high, ranks, preferred_element_type=jnp.float32)
        + jnp.dot(middle, ranks, preferred_element_type=jnp.float32)
    ) + jnp.dot(low, ranks, preferred_element_type=jnp.float32)
    own = lax.broadcasted_iota(jnp.int32, (owners, row_count), 0) == ids_ref[...]
    out_ref[...] = jnp.reshape(jnp.sum(jnp.where(own, by_rank, 0.0), axis=0, keepdims=True), out_ref.shape)


def collect(scores, ranks, ids):
    return pl.pallas_call(
        collect_kernel,
        out_shape=jax.ShapeDtypeStruct((ranks.shape[1],), jnp.float32),
        in_specs=vmem(3),
        out_specs=pl.BlockSpec(memory_space=pltpu.VMEM),
        compiler_params=params(),
    )(scores, ranks, ids)


def steps_of(owners):
    if owners == 8:
        return (0, 6, 5, 3, 7, 1, 2, 4)
    return tuple(range(owners))


def swap(block, axis, step, size):
    if step == 0:
        return block
    return lax.ppermute(block, axis, [(i, i ^ step) for i in range(size)])


def direct_shards(embeddings, cluster_ids):
    owners = lax.axis_size("blk")
    capacity = 2 * embeddings.shape[0] // owners
    me = jnp.reshape(lax.axis_index("blk").astype(jnp.int32), (1,))
    blocks, ranks, ids = prepare(me, embeddings, cluster_ids, owners, capacity)
    own_blocks = [None] * owners
    for k, step in enumerate(steps_of(owners)):
        own_blocks[k] = swap(blocks[k], "blk", step, owners)
    other_blocks = [swap(block, "pair", 1, 2) for block in own_blocks]
    joined, total = own_sums(own_blocks)
    scores = cross_scores(me, other_blocks, joined, total)
    returned = lax.all_to_all(scores, "blk", split_axis=0, concat_axis=0, tiled=True)
    return collect(returned, ranks, ids)


def unit_vectors(values):
    widened = values.astype(jnp.float32)
    scale = lax.rsqrt(jnp.sum(widened * widened, axis=1, keepdims=True) + EPSILON)
    return (widened * scale).astype(jnp.bfloat16)


def wide_shards(embeddings, cluster_ids):
    row_count, width = embeddings.shape
    owners = lax.axis_size("blk")
    capacity = 2 * row_count // owners
    slots = owners * capacity
    units = unit_vectors(embeddings)
    marks = (cluster_ids[:, None] == jnp.arange(owners, dtype=jnp.int32)[None, :]).astype(jnp.bfloat16)
    row_order = jnp.arange(row_count, dtype=jnp.int32)
    earlier = (row_order[:, None] > row_order[None, :]).astype(jnp.bfloat16)
    before = jnp.dot(earlier, marks, preferred_element_type=jnp.float32)
    rank = jnp.sum(before * marks.astype(jnp.float32), axis=1).astype(jnp.int32)
    target = cluster_ids * capacity + rank
    empty_row = jnp.where(jnp.arange(width) == 0, EMPTY_MARK, 0.0).astype(jnp.bfloat16)
    send = jnp.broadcast_to(empty_row[None, :], (slots, width)).at[target].set(units)
    own = lax.all_to_all(
        send.reshape(owners, capacity, width), "blk", split_axis=0, concat_axis=0, tiled=True
    ).reshape(slots, width)
    other = lax.ppermute(own, "pair", [(0, 1), (1, 0)])
    columns = jnp.concatenate([own, other], axis=0)
    living = columns[:, 0].astype(jnp.float32) < EMPTY_ABOVE
    products = lax.dot_general(own, columns, (((1,), (1,)), ((), ())), preferred_element_type=jnp.float32)
    position = jnp.arange(2 * slots, dtype=jnp.int32)
    keep = living[None, :] & (position[:slots, None] != position[None, :])
    density = jnp.sum(jnp.where(keep, jnp.exp(products * SHARPNESS), 0.0), axis=1)
    scores = jnp.log(jnp.where(living[:slots], density, 1.0)).reshape(owners, capacity)
    returned = lax.all_to_all(scores, "blk", split_axis=0, concat_axis=0, tiled=True)
    return returned.reshape(slots)[target]


def solution(mesh):
    placed = (P(("groups", "blk", "pair"), None), P(("groups", "blk", "pair")))
    shards = direct_shards if mesh.shape["blk"] <= DIRECT_OWNERS else wide_shards
    return jax.shard_map(
        shards, mesh=mesh, in_specs=placed, out_specs=P(("groups", "blk", "pair")), check_vma=False
    )
```

```python
import functools
import math

import jax
import jax.numpy as jnp
from jax import lax
from jax.experimental import pallas as pl
from jax.experimental.pallas import tpu as pltpu
from jax.sharding import PartitionSpec as P

SHARPNESS = 10.0
SHARPNESS_LOG2 = SHARPNESS * math.log2(math.e)
EPSILON = 1e-06
EMPTY_MARK = 2.0
EMPTY_ABOVE = 1.5
DIRECT_OWNERS = 8
SCORE_LANES = 128
COLUMNS = 256


def vmem(count):
    return [pl.BlockSpec(memory_space=pltpu.VMEM)] * count


def params(mib=24):
    return pltpu.CompilerParams(vmem_limit_bytes=mib * 1024 * 1024)


def prepare_kernel(owners, capacity, me_ref, rows_hbm, ids_hbm, *refs):
    block_refs = refs[:owners]
    ranks_ref, ids_row_ref, pick_ref, rows_ref, ids_ref, sems = refs[owners:]
    ids_copy = pltpu.make_async_copy(ids_hbm, ids_ref, sems.at[0])
    rows_copy = pltpu.make_async_copy(rows_hbm, rows_ref, sems.at[1])
    ids_copy.start()
    rows_copy.start()
    row_count = ids_ref.shape[0]
    above = lax.broadcasted_iota(jnp.int32, (row_count, row_count), 0)
    right = lax.broadcasted_iota(jnp.int32, (row_count, row_count), 1)
    earlier = jnp.where(above < right, 1.0, 0.0).astype(jnp.bfloat16)
    labels = lax.broadcasted_iota(jnp.int32, (owners, row_count), 0)
    ids_copy.wait()
    ids = jnp.reshape(ids_ref[...], (1, row_count))
    ids_row_ref[...] = ids
    step = ids ^ me_ref[0]
    relative = sum(jnp.where(step == value, k, 0) for k, value in enumerate(steps_of(owners)))
    inside = (labels == relative).astype(jnp.float32)
    before = jnp.dot(inside.astype(jnp.bfloat16), earlier, preferred_element_type=jnp.float32)
    rank = jnp.sum(before * inside, axis=0, keepdims=True).astype(jnp.int32)
    slot = relative * capacity + rank
    slots = owners * capacity
    pick_ref[...] = jnp.where(
        lax.broadcasted_iota(jnp.int32, (slots, row_count), 0) == slot, 1.0, 0.0
    ).astype(jnp.bfloat16)
    ranks_ref[...] = jnp.where(
        lax.broadcasted_iota(jnp.int32, (capacity, row_count), 0) == rank, 1.0, 0.0
    ).astype(jnp.bfloat16)
    counts = jnp.broadcast_to(jnp.sum(inside, axis=1, keepdims=True), (owners, 128))
    first = lax.broadcasted_iota(jnp.int32, (owners, 128), 1) == 0
    marks = jnp.where(first & (counts == 0.0), EMPTY_MARK, 0.0)
    rows_copy.wait()
    values = rows_ref[...].astype(jnp.float32)
    scale = lax.rsqrt(jnp.sum(values * values, axis=1, keepdims=True) + EPSILON)
    units = (values * scale).astype(jnp.bfloat16)
    width = units.shape[1]
    for left in range(0, width, COLUMNS):
        right = min(left + COLUMNS, width)
        columns = jnp.dot(pick_ref[...], units[:, left:right], preferred_element_type=jnp.float32)
        for k, block_ref in enumerate(block_refs):
            block = columns[k * capacity:(k + 1) * capacity]
            if left == 0:
                block_ref[:, 0:128] = (block[:, 0:128] + marks[k:k + 1, :]).astype(jnp.bfloat16)
                block_ref[:, 128:right] = block[:, 128:].astype(jnp.bfloat16)
            else:
                block_ref[:, left:right] = block.astype(jnp.bfloat16)


def prepare(me, rows, ids, owners, capacity):
    row_count, width = rows.shape
    *blocks, ranks, ids_row = pl.pallas_call(
        functools.partial(prepare_kernel, owners, capacity),
        out_shape=[jax.ShapeDtypeStruct((capacity, width), jnp.bfloat16)] * owners
        + [
            jax.ShapeDtypeStruct((capacity, row_count), jnp.bfloat16),
            jax.ShapeDtypeStruct((1, row_count), jnp.int32),
        ],
        in_specs=[pl.BlockSpec(memory_space=pltpu.SMEM)] + [pl.BlockSpec(memory_space=pltpu.HBM)] * 2,
        out_specs=vmem(owners + 2),
        scratch_shapes=[
            pltpu.VMEM((owners * capacity, row_count), jnp.bfloat16),
            pltpu.VMEM(rows.shape, rows.dtype),
            pltpu.VMEM(ids.shape, ids.dtype),
            pltpu.SemaphoreType.DMA((2,)),
        ],
        compiler_params=params(),
    )(
        me,
        pltpu.with_memory_space_constraint(rows, pltpu.HBM),
        pltpu.with_memory_space_constraint(ids, pltpu.HBM),
    )
    return blocks, ranks, ids_row


def partial_sums(own, others, others_refs, own_block):
    capacity = others_refs[0].shape[0]
    count = own.shape[0]
    total = jnp.zeros((1, count), jnp.float32)
    products = lax.dot_general(others, own, (((1,), (1,)), ((), ())), preferred_element_type=jnp.float32)
    for k, block_ref in enumerate(others_refs):
        powers = jnp.exp2(products[k * capacity:(k + 1) * capacity] * SHARPNESS_LOG2)
        if own_block:
            row = lax.broadcasted_iota(jnp.int32, powers.shape, 0) + k * capacity
            powers = jnp.where(row == lax.broadcasted_iota(jnp.int32, powers.shape, 1), 0.0, powers)
        living = block_ref[0:16, 0:128].astype(jnp.float32)[0:1, 0:1] < EMPTY_ABOVE
        total = total + jnp.where(living, jnp.sum(powers, axis=0, keepdims=True), 0.0)
    return total


def own_kernel(owners, *refs):
    block_refs, joined_ref, total_ref = refs[:owners], refs[owners], refs[owners + 1]
    capacity = block_refs[0].shape[0]
    for k, block_ref in enumerate(block_refs):
        joined_ref[k * capacity:(k + 1) * capacity, :] = block_ref[...]
    own = joined_ref[...]
    total_ref[...] = partial_sums(own, own, block_refs, True)


def own_sums(blocks):
    capacity, width = blocks[0].shape
    slots = len(blocks) * capacity
    return pl.pallas_call(
        functools.partial(own_kernel, len(blocks)),
        out_shape=[
            jax.ShapeDtypeStruct((slots, width), jnp.bfloat16),
            jax.ShapeDtypeStruct((1, slots), jnp.float32),
        ],
        in_specs=vmem(len(blocks)),
        out_specs=vmem(2),
        compiler_params=params(),
        cost_estimate=pl.CostEstimate(
            flops=2 * slots * slots * width, bytes_accessed=4 * slots * width, transcendentals=slots * slots
        ),
    )(*blocks)


def cross_kernel(owners, me_ref, *refs):
    block_refs, joined_ref, total_ref, score_ref, others_ref = refs[:owners], *refs[owners:]
    me = me_ref[0]
    capacity = block_refs[0].shape[0]
    for k, block_ref in enumerate(block_refs):
        others_ref[k * capacity:(k + 1) * capacity, :] = block_ref[...]
    total = total_ref[...] + partial_sums(joined_ref[...], others_ref[...], block_refs, False)
    scores = jnp.log(jnp.where(total > 0.0, total, 1.0))
    for k, step in enumerate(steps_of(owners)):
        score_ref[pl.ds(me ^ step, 1), 0:capacity] = scores[:, k * capacity:(k + 1) * capacity]


def cross_scores(me, blocks, joined, total):
    capacity, width = blocks[0].shape
    slots = len(blocks) * capacity
    return pl.pallas_call(
        functools.partial(cross_kernel, len(blocks)),
        out_shape=jax.ShapeDtypeStruct((len(blocks), SCORE_LANES), jnp.float32),
        in_specs=[pl.BlockSpec(memory_space=pltpu.SMEM)] + vmem(len(blocks) + 2),
        out_specs=pl.BlockSpec(memory_space=pltpu.VMEM),
        scratch_shapes=[pltpu.VMEM((slots, width), jnp.bfloat16)],
        compiler_params=params(),
    )(me, *blocks, joined, total)


def collect_kernel(score_ref, ranks_ref, ids_ref, out_ref):
    owners = score_ref.shape[0]
    capacity, row_count = ranks_ref.shape
    scores = score_ref[:, 0:capacity]
    high = scores.astype(jnp.bfloat16)
    rest = scores - high.astype(jnp.float32)
    middle = rest.astype(jnp.bfloat16)
    low = (rest - middle.astype(jnp.float32)).astype(jnp.bfloat16)
    ranks = ranks_ref[...]
    by_rank = (
        jnp.dot(high, ranks, preferred_element_type=jnp.float32)
        + jnp.dot(middle, ranks, preferred_element_type=jnp.float32)
    ) + jnp.dot(low, ranks, preferred_element_type=jnp.float32)
    own = lax.broadcasted_iota(jnp.int32, (owners, row_count), 0) == ids_ref[...]
    out_ref[...] = jnp.reshape(jnp.sum(jnp.where(own, by_rank, 0.0), axis=0, keepdims=True), out_ref.shape)


def collect(scores, ranks, ids):
    return pl.pallas_call(
        collect_kernel,
        out_shape=jax.ShapeDtypeStruct((ranks.shape[1],), jnp.float32),
        in_specs=vmem(3),
        out_specs=pl.BlockSpec(memory_space=pltpu.VMEM),
        compiler_params=params(),
    )(scores, ranks, ids)


def steps_of(owners):
    if owners == 8:
        return (0, 6, 5, 1, 7, 3, 2, 4)
    return tuple(range(owners))


def swap(block, axis, step, size):
    if step == 0:
        return block
    return lax.ppermute(block, axis, [(i, i ^ step) for i in range(size)])


def direct_shards(embeddings, cluster_ids):
    owners = lax.axis_size("blk")
    capacity = 2 * embeddings.shape[0] // owners
    me = jnp.reshape(lax.axis_index("blk").astype(jnp.int32), (1,))
    blocks, ranks, ids = prepare(me, embeddings, cluster_ids, owners, capacity)
    own_blocks = [None] * owners
    for k, step in enumerate(steps_of(owners)):
        own_blocks[k] = swap(blocks[k], "blk", step, owners)
    other_blocks = [swap(block, "pair", 1, 2) for block in own_blocks]
    joined, total = own_sums(own_blocks)
    scores = cross_scores(me, other_blocks, joined, total)
    returned = lax.all_to_all(scores, "blk", split_axis=0, concat_axis=0, tiled=True)
    return collect(returned, ranks, ids)


def unit_vectors(values):
    widened = values.astype(jnp.float32)
    scale = lax.rsqrt(jnp.sum(widened * widened, axis=1, keepdims=True) + EPSILON)
    return (widened * scale).astype(jnp.bfloat16)


def wide_shards(embeddings, cluster_ids):
    row_count, width = embeddings.shape
    owners = lax.axis_size("blk")
    capacity = 2 * row_count // owners
    slots = owners * capacity
    units = unit_vectors(embeddings)
    marks = (cluster_ids[:, None] == jnp.arange(owners, dtype=jnp.int32)[None, :]).astype(jnp.bfloat16)
    row_order = jnp.arange(row_count, dtype=jnp.int32)
    earlier = (row_order[:, None] > row_order[None, :]).astype(jnp.bfloat16)
    before = jnp.dot(earlier, marks, preferred_element_type=jnp.float32)
    rank = jnp.sum(before * marks.astype(jnp.float32), axis=1).astype(jnp.int32)
    target = cluster_ids * capacity + rank
    empty_row = jnp.where(jnp.arange(width) == 0, EMPTY_MARK, 0.0).astype(jnp.bfloat16)
    send = jnp.broadcast_to(empty_row[None, :], (slots, width)).at[target].set(units)
    own = lax.all_to_all(
        send.reshape(owners, capacity, width), "blk", split_axis=0, concat_axis=0, tiled=True
    ).reshape(slots, width)
    other = lax.ppermute(own, "pair", [(0, 1), (1, 0)])
    columns = jnp.concatenate([own, other], axis=0)
    living = columns[:, 0].astype(jnp.float32) < EMPTY_ABOVE
    products = lax.dot_general(own, columns, (((1,), (1,)), ((), ())), preferred_element_type=jnp.float32)
    position = jnp.arange(2 * slots, dtype=jnp.int32)
    keep = living[None, :] & (position[:slots, None] != position[None, :])
    density = jnp.sum(jnp.where(keep, jnp.exp(products * SHARPNESS), 0.0), axis=1)
    scores = jnp.log(jnp.where(living[:slots], density, 1.0)).reshape(owners, capacity)
    returned = lax.all_to_all(scores, "blk", split_axis=0, concat_axis=0, tiled=True)
    return returned.reshape(slots)[target]


def solution(mesh):
    placed = (P(("groups", "blk", "pair"), None), P(("groups", "blk", "pair")))
    shards = direct_shards if mesh.shape["blk"] <= DIRECT_OWNERS else wide_shards
    return jax.shard_map(
        shards, mesh=mesh, in_specs=placed, out_specs=P(("groups", "blk", "pair")), check_vma=False
    )
```
